512 devices in a mesh: shard: 128 (over z, x, core), help: 4 (over y).
Axes of the slice: x: 4, y: 4, z: 16, core: 2. Of those that a mesh axis runs over, the one named last changes fastest.
Arguments:
- embeds: bfloat16 [65536, 4096], P(('shard', 'help')), may hold values from -6 to 6
- head_rows: bfloat16 [4096, 256], replicated, may hold values from -0.09375 to 0.09375
- cluster_of: int32 [65536], P(('shard', 'help')), may hold values from 0 to 2047, as said below
- owner_of: int32 [2048], replicated, may hold values from 0 to 127, as said below
- live_mask: int32 [65536], P(('shard', 'help')), may hold values 0 or 1
Outputs:
- prefix: bfloat16 [65536, 256], P(('shard', 'help'))
- nearest: float32 [65536], P(('shard', 'help'))
The draws below stay inside these ranges and needn't reach their ends.
Inputs may be any that keep to these rules, and one draw needn't show every extreme that they name: `cluster_of`: counting rows by the owner (owner_of) of their cluster, the 128 rows of one device include at most 2 rows for any one owner, and exactly 2 for some owner on every device. `owner_of`: every owner holds exactly 16 clusters.
All inputs are finite; a program needn't handle non-finite values. No bound on the sum of `live_mask` on one device may be relied on, other than what follows from the above.
Results may differ from the reference program's by a relative error of at most 0.0011.
Values may be sent and summed in bfloat16 or wider, within the bound.
No kernel may reach another device: no remote copies, remote signals or barrier semaphores. Data moves between devices by JAX's collectives and lax.ppermute only.
A program may use at most 64 MiB of HBM per device.

```python
import jax
import jax.numpy as jnp
from jax import lax

D = 4096
PREFIX = 256
ROWS_DEV = 128
CLU_DEV = 16
SLOTS = 2
ROWS = 65536
CLUSTERS = 2048
N_SHARD = 128
N_HELP = 4


def owner_perm(key):
    return jax.random.permutation(jax.random.fold_in(key, 101), CLUSTERS)


def draw_owner_of(key, part):
    shuffled = owner_perm(key)
    return (shuffled // CLU_DEV).astype(jnp.int32)


def draw_cluster_of(key, part):
    shuffled = owner_perm(key)
    inverse = jnp.argsort(shuffled).astype(jnp.int32)
    key = jax.random.fold_in(key, 7)
    device_total = ROWS // ROWS_DEV
    pool_size = N_SHARD * SLOTS
    key_bias, key_rank, key_force, key_order, key_local = jax.random.split(key, 5)
    owner_bias = jax.random.randint(key_bias, (N_SHARD,), 0, pool_size)
    slot_ranks = jax.vmap(lambda k: jax.random.permutation(k, pool_size))(jax.random.split(key_rank, device_total))
    forced = jax.random.randint(key_force, (device_total, 1), 0, N_SHARD)
    slot_owner = jnp.arange(pool_size, dtype=jnp.int32) // SLOTS
    slot_score = slot_ranks + owner_bias[slot_owner][None, :] - jnp.where(slot_owner[None, :] == forced, 4 * pool_size, 0)
    slot_score = slot_score * pool_size + slot_ranks
    chosen = jnp.argsort(slot_score, axis=1)[:, :ROWS_DEV].astype(jnp.int32)
    shuffle = jax.vmap(lambda k: jax.random.permutation(k, ROWS_DEV))(jax.random.split(key_order, device_total))
    chosen = jnp.take_along_axis(chosen, shuffle, axis=1)
    owner_row = chosen // SLOTS
    local_rank = jax.random.randint(key_local, (device_total, ROWS_DEV), 0, CLU_DEV)
    return inverse[owner_row * CLU_DEV + local_rank].reshape(ROWS).astype(jnp.int32)


def with_ends(values, rng, least, top_value):
    longest = values.shape.index(max(values.shape))
    spots = []
    for shift in (0, 1):
        where = [jax.random.randint(jax.random.fold_in(rng, axis), (), 0, length) for axis, length in enumerate(values.shape)]
        where[longest] = (where[longest] + shift) % values.shape[longest]
        spots.append(tuple(where))
    return values.at[spots[0]].set(least).at[spots[1]].set(top_value)


def level_of(rng, extent, cuts, smallest, high):
    loudness, own = 1.0, jax.random.fold_in(rng, 6)
    for position, blocks in cuts:
        draws = jnp.exp(jax.random.uniform(jax.random.fold_in(own, position), (blocks,), jnp.float32, smallest / len(cuts), high / len(cuts)))
        loudness = loudness * jnp.repeat(draws, extent[position] // blocks).reshape([-1 if axis == position else 1 for axis in range(len(extent))])
    return loudness


def scatter_about(key, dims, width, most, cuts=(), kind=jnp.bfloat16):
    values = width * jax.random.normal(key, dims, jnp.float32)
    if cuts:
        values = values * level_of(key, dims, cuts, -0.22, 0.18)
    return jnp.clip(values, -most, most).astype(kind)


def setup_inputs(seed: int = 0) -> dict:
    keys = jax.random.split(jax.random.key(seed), 6)
    embeds = scatter_about(keys[0], (ROWS, D), 1.0, 6.0, ((0, 512),))
    head_rows = scatter_about(keys[1], (D, PREFIX), D ** -0.5, 0.09375)
    cluster_of = draw_cluster_of(jax.random.fold_in(keys[5], 71), 0)
    owner_of = draw_owner_of(jax.random.fold_in(keys[5], 71), 0)
    live_mask = with_ends((jax.random.randint(keys[4], (ROWS,), 0, 8) < 7).astype(jnp.int32), jax.random.fold_in(keys[4], 1), 0, 1)
    return {"embeds": embeds, "head_rows": head_rows, "cluster_of": cluster_of, "owner_of": owner_of, "live_mask": live_mask}


NORM_EPS = 1e-06

def reference(embeds, head_rows, cluster_of, owner_of, live_mask):
    projected = jnp.dot(embeds, head_rows, preferred_element_type=jnp.float32)
    prefix = (projected * lax.rsqrt(lax.optimization_barrier(jnp.sum(projected * projected, axis=1, keepdims=True)) + NORM_EPS)).astype(jnp.bfloat16)
    row_count = prefix.shape[0]
    row_ids = jnp.arange(row_count, dtype=jnp.int32)
    device_id = row_ids // ROWS_DEV
    owner_row = owner_of[cluster_of].astype(jnp.int32)
    group_key = device_id * N_SHARD + owner_row
    row_order = jnp.argsort(group_key, stable=True).astype(jnp.int32)
    sorted_key = group_key[row_order]
    first_pos = jnp.searchsorted(sorted_key, sorted_key, side='left').astype(jnp.int32)
    slot_sorted = jnp.arange(row_count, dtype=jnp.int32) - first_pos
    slot_pos = jnp.zeros((row_count,), jnp.int32).at[row_order].set(slot_sorted)
    source_shard = device_id // N_HELP
    source_help = device_id % N_HELP
    slab_width = N_HELP * N_SHARD * SLOTS
    slot_index = source_help * (N_SHARD * SLOTS) + source_shard * SLOTS + slot_pos
    slot_table = jnp.full((N_SHARD, slab_width), row_count, jnp.int32).at[owner_row, slot_index].set(row_ids)
    row_label = jnp.where(live_mask == 1, cluster_of, -1).astype(jnp.int32)
    padded = jnp.concatenate([prefix.astype(jnp.float32), jnp.zeros((1, prefix.shape[1]), jnp.float32)], axis=0)
    labels = jnp.concatenate([row_label, jnp.full((1,), -1, jnp.int32)], axis=0)

    def owner_best(row_index):
        members = padded[row_index]
        member_label = labels[row_index]
        scores = jnp.dot(members, members.T, precision=lax.Precision.HIGHEST)
        allowed = (member_label[:, None] == member_label[None, :]) & (member_label[:, None] >= 0)
        allowed = allowed & (member_label[None, :] >= 0) & (row_index[:, None] != row_index[None, :])
        return lax.optimization_barrier(jnp.max(jnp.where(allowed, scores, jnp.float32(-1.0)), axis=1))
    best_cos = lax.map(owner_best, slot_table)
    spread = jnp.zeros((row_count + 1,), jnp.float32).at[slot_table.reshape(-1)].set(best_cos.reshape(-1))
    nearest = jnp.where(live_mask == 1, spread[:row_count], jnp.float32(-1.0))
    return (prefix, nearest)
```

```python
import functools

import jax
import jax.numpy as jnp
from jax import lax
from jax.experimental import pallas as pl
from jax.experimental.pallas import tpu as pltpu
from jax.sharding import Mesh, PartitionSpec as P

NORM_EPS = 1e-06
LANES = 128
PLANES = 16
COLUMNS = 8
HELPERS = 4
SLOTS = 2
PLANE_SLOTS = COLUMNS * SLOTS
SLAB = PLANES * PLANE_SLOTS
OWNER_SLOTS = PLANES * SLOTS
CHUNKS = 4

F32 = jnp.float32
BF16 = jnp.bfloat16


def iota(shape, dim):
    return lax.broadcasted_iota(jnp.int32, shape, dim)


def hot(condition):
    return jnp.where(condition, 1.0, 0.0).astype(BF16)


def dot_nt(left, right):
    return lax.dot_general(left, right, (((1,), (1,)), ((), ())), preferred_element_type=F32)


def dot(left, right):
    return jnp.dot(left, right, preferred_element_type=F32)


def project_kernel(
    embeds, head, cluster_ref, owner_ref, live_ref, prefix_ref, send_ref, target_ref,
    embeds_buf, head_buf, embeds_sem, head_sem,
):
    depth = head_buf.shape[1]
    copies = []
    for part in range(CHUNKS):
        span = pl.ds(part * depth, depth)
        pair = (
            pltpu.make_async_copy(head.at[span, :], head_buf.at[part], head_sem.at[part]),
            pltpu.make_async_copy(embeds.at[:, span], embeds_buf.at[part], embeds_sem.at[part]),
        )
        for copy in pair:
            copy.start()
        copies.append(pair)

    square = (LANES, LANES)
    cluster = cluster_ref[...]
    high, low = cluster >> 7, cluster & 127
    by_low = dot(owner_ref[...].astype(F32).astype(BF16), hot(iota(square, 0) == low))
    owner = jnp.sum(jnp.where(iota(by_low.shape, 0) == high, by_low, 0.0), axis=0, keepdims=True)
    owner = owner.astype(jnp.int32)
    owner_hot = hot(iota(square, 0) == owner)
    same = lax.dot_general(
        owner_hot, owner_hot, (((0,), (0,)), ((), ())), preferred_element_type=F32
    )
    slot = jnp.sum(jnp.where(iota(square, 0) < iota(square, 1), same, 0.0), axis=0, keepdims=True)
    target = owner * SLOTS + slot.astype(jnp.int32)
    target_ref[...] = jnp.broadcast_to(target, target_ref.shape)

    live = live_ref[...] == 1
    high_label = jnp.where(live, high + 1, 0)
    low_label = jnp.where(live, low, 0)
    line = iota(square, 0)
    part = jnp.where((line & 7) == 0, high_label, jnp.where((line & 7) == 1, low_label, 0))
    part = jnp.where((line >> 3) == (target >> 4), part, 0).astype(F32).astype(BF16)
    labels = dot_nt(part, hot(line == (target & 15))).reshape(PLANES, 8, LANES)
    hit = hot(iota((SLAB, LANES), 0) == target)

    projected = jnp.zeros(prefix_ref.shape, F32)
    for part, pair in enumerate(copies):
        for copy in pair:
            copy.wait()
        projected += dot(embeds_buf[part], head_buf[part])
    norm = lax.rsqrt(jnp.sum(projected * projected, axis=1, keepdims=True) + NORM_EPS)
    prefix = (projected * norm).astype(BF16)
    prefix_ref[...] = prefix
    rows = dot(hit, prefix).reshape(PLANES, PLANE_SLOTS, 2 * LANES)
    send_ref[...] = jnp.concatenate(
        [rows[:, :, :LANES], rows[:, :, LANES:], labels], axis=1
    ).astype(BF16)


def sort_kernel(got_ref, send_ref):
    got = got_ref[...].astype(F32)
    low = got[:, :PLANE_SLOTS].reshape(SLAB, LANES).astype(BF16)
    high = got[:, PLANE_SLOTS : 2 * PLANE_SLOTS].reshape(SLAB, LANES).astype(BF16)
    dest = iota((SLAB, SLAB), 0)
    source = ((dest >> 1) & 15) * PLANE_SLOTS + (dest >> 5) * SLOTS + (dest & 1)
    order = hot(iota((SLAB, SLAB), 1) == source)
    rows = dot(order, jnp.concatenate([low, high], axis=1))
    rows = rows.reshape(COLUMNS, OWNER_SLOTS, 2 * LANES)

    square = (LANES, LANES)
    tiles = got[:, 2 * PLANE_SLOTS :].reshape(PLANES * 8, LANES).astype(BF16)
    line, lane = iota(square, 0), iota(square, 1)
    pick = ((line & 31) >> 1) * 8 + (line >> 5)
    spread = dot(hot((lane == pick) & (line < 2 * OWNER_SLOTS)), tiles)
    spread = jnp.where((lane & 1) == (line & 1), spread, 0.0).astype(BF16)
    group = (COLUMNS * 8, LANES)
    labels = dot_nt(hot((iota(group, 1) >> 1) == (iota(group, 0) >> 3)), spread)
    labels = labels.reshape(COLUMNS, 8, LANES)
    out = jnp.concatenate([rows[:, :, :LANES], rows[:, :, LANES:], labels], axis=1).astype(BF16)
    for helper in range(HELPERS):
        send_ref[:, helper] = out


def best_kernel(got_ref, out_ref):
    helper = lax.axis_index("help")
    sources = COLUMNS * HELPERS
    total = sources * OWNER_SLOTS
    low = got_ref[:, :, :OWNER_SLOTS].reshape(total, LANES)
    high = got_ref[:, :, OWNER_SLOTS : 2 * OWNER_SLOTS].reshape(total, LANES)
    columns = jnp.concatenate([low, high], axis=1)
    own_low = got_ref[:, helper, :OWNER_SLOTS].reshape(SLAB, LANES)
    own_high = got_ref[:, helper, OWNER_SLOTS : 2 * OWNER_SLOTS].reshape(SLAB, LANES)

    dest = iota((SLAB, SLAB), 0)
    in_owner = ((dest >> 3) & 15) * SLOTS + (dest >> 7)
    order = hot(iota((SLAB, SLAB), 1) == (dest & 7) * OWNER_SLOTS + in_owner)
    own = dot(order, jnp.concatenate([own_low, own_high], axis=1)).astype(BF16)
    scores = dot_nt(own, columns)

    tiles = got_ref[...].astype(F32)[:, :, 2 * OWNER_SLOTS :].reshape(sources * 8, LANES).astype(BF16)
    shape = (total, sources * 8)
    spread = dot(hot(iota(shape, 1) == (iota(shape, 0) >> 5) * 8), tiles)
    line, lane = iota((total, LANES), 0) & 31, iota((total, LANES), 1)
    spread = jnp.where(lane == line, spread * 128.0, jnp.where(lane == line + 32, spread, 0.0))
    column_label = dot_nt(jnp.ones((8, LANES), BF16), spread.astype(BF16))[:1]

    shape = (SLAB, sources * 8)
    line = iota(shape, 0)
    own_spread = dot(hot(iota(shape, 1) == ((line & 7) * HELPERS + helper) * 8), tiles)
    line, lane = iota((SLAB, LANES), 0), iota((SLAB, LANES), 1)
    line = ((line >> 3) & 15) * SLOTS + (line >> 7)
    own_label = jnp.sum(
        jnp.where(lane == line, own_spread * 128.0, jnp.where(lane == line + 32, own_spread, 0.0)),
        axis=1,
        keepdims=True,
    )
    own_label = jnp.where(own_label > 0.5, own_label, -1.0)
    line = iota((SLAB, 1), 0)
    own_index = ((line & 7) * HELPERS + helper) * OWNER_SLOTS + ((line >> 3) & 15) * SLOTS + (line >> 7)
    allowed = (own_label == column_label) & (own_index != iota((SLAB, total), 1))
    best = jnp.max(jnp.where(allowed, scores, -1.0), axis=1, keepdims=True)
    half = SLAB // 2
    lane = iota(out_ref.shape, 1)
    out_ref[...] = jnp.where(lane == 0, best[:half], jnp.where(lane == 1, best[half:], 0.0))


def finish_kernel(got_ref, target_ref, live_ref, out_ref):
    got = got_ref[...]
    target = target_ref[:1]
    value = jnp.where((target & 1) == 0, got[:, 0:1], got[:, 1:2])
    value = jnp.where(iota(got.shape, 0) == (target >> 1), value, 0.0)
    value = jnp.sum(value, axis=0, keepdims=True)
    out_ref[...] = jnp.where(live_ref[...] == 1, value, -1.0)


VMEM = pl.BlockSpec(memory_space=pltpu.VMEM)
ANY = pl.BlockSpec(memory_space=pl.ANY)
LIMIT = pltpu.CompilerParams(vmem_limit_bytes=32 * 1024 * 1024)


def shards(embeds, head_rows, cluster_of, owner_of, live_mask):
    row_count, width = embeds.shape
    depth = width // CHUNKS
    live = live_mask.reshape(1, row_count)
    prefix, send, target = pl.pallas_call(
        project_kernel,
        out_shape=(
            jax.ShapeDtypeStruct((row_count, 2 * LANES), BF16),
            jax.ShapeDtypeStruct((PLANES, 2 * PLANE_SLOTS + 8, LANES), BF16),
            jax.ShapeDtypeStruct((8, row_count), jnp.int32),
        ),
        in_specs=[ANY, ANY, VMEM, VMEM, VMEM],
        out_specs=(VMEM, VMEM, VMEM),
        scratch_shapes=[
            pltpu.VMEM((CHUNKS, row_count, depth), BF16),
            pltpu.VMEM((CHUNKS, depth, 2 * LANES), BF16),
            pltpu.SemaphoreType.DMA((CHUNKS,)),
            pltpu.SemaphoreType.DMA((CHUNKS,)),
        ],
        compiler_params=LIMIT,
        name="project",
    )(embeds, head_rows, cluster_of.reshape(1, row_count), owner_of.reshape(-1, LANES), live)
    got = lax.all_to_all(send, "z", split_axis=0, concat_axis=0, tiled=True)
    lines = 2 * OWNER_SLOTS + 8
    send = pl.pallas_call(
        sort_kernel,
        out_shape=jax.ShapeDtypeStruct((COLUMNS, HELPERS, lines, LANES), BF16),
        in_specs=[VMEM],
        out_specs=VMEM,
        compiler_params=LIMIT,
        name="sort",
    )(got)
    got = lax.all_to_all(
        send.reshape(COLUMNS * HELPERS, lines, LANES),
        ("x", "core", "help"),
        split_axis=0,
        concat_axis=0,
        tiled=True,
    )
    best = pl.pallas_call(
        best_kernel,
        out_shape=jax.ShapeDtypeStruct((PLANES * COLUMNS, LANES), F32),
        in_specs=[VMEM],
        out_specs=VMEM,
        compiler_params=LIMIT,
        name="best",
    )(got.reshape(COLUMNS, HELPERS, lines, LANES))
    back = lax.all_to_all(best, ("z", "x", "core"), split_axis=0, concat_axis=0, tiled=True)
    nearest = pl.pallas_call(
        finish_kernel,
        out_shape=jax.ShapeDtypeStruct((1, row_count), F32),
        in_specs=[VMEM, VMEM, VMEM],
        out_specs=VMEM,
        compiler_params=LIMIT,
        name="finish",
    )(back, target, live)
    return (prefix, nearest.reshape(row_count))


def solution(mesh):
    axes = ("z", "x", "core", "help")
    fine = Mesh(mesh.devices.reshape(PLANES, 4, 2, HELPERS), axes)
    return jax.shard_map(
        shards,
        mesh=fine,
        in_specs=(P(axes, None), P(), P(axes), P(), P(axes)),
        out_specs=(P(axes, None), P(axes)),
        check_vma=False,
    )
```

```python
import functools

import jax
import jax.numpy as jnp
from jax import lax
from jax.experimental import pallas as pl
from jax.experimental.pallas import tpu as pltpu
from jax.sharding import Mesh, PartitionSpec as P

NORM_EPS = 1e-06
LANES = 128
PLANES = 16
COLUMNS = 8
HELPERS = 4
SLOTS = 2
PLANE_SLOTS = COLUMNS * SLOTS
SLAB = PLANES * PLANE_SLOTS
OWNER_SLOTS = PLANES * SLOTS
CHUNKS = 4

F32 = jnp.float32
BF16 = jnp.bfloat16


def iota(shape, dim):
    return lax.broadcasted_iota(jnp.int32, shape, dim)


def hot(condition):
    return jnp.where(condition, 1.0, 0.0).astype(BF16)


def dot_nt(left, right):
    return lax.dot_general(left, right, (((1,), (1,)), ((), ())), preferred_element_type=F32)


def dot(left, right):
    return jnp.dot(left, right, preferred_element_type=F32)


def project_kernel(
    embeds, head, cluster, owner_of, live_mask, prefix_ref, send_ref, target_ref,
    embeds_buf, head_buf, cluster_ref, owner_ref, live_ref, embeds_sem, head_sem, index_sem,
):
    depth = head_buf.shape[1]
    index_copies = [
        pltpu.make_async_copy(source, buf, index_sem.at[spot])
        for spot, (source, buf) in enumerate(
            ((cluster, cluster_ref), (owner_of, owner_ref), (live_mask, live_ref))
        )
    ]
    for copy in index_copies:
        copy.start()
    copies = []
    for part in range(CHUNKS):
        span = pl.ds(part * depth, depth)
        pair = (
            pltpu.make_async_copy(head.at[span, :], head_buf.at[part], head_sem.at[part]),
            pltpu.make_async_copy(embeds.at[:, span], embeds_buf.at[part], embeds_sem.at[part]),
        )
        for copy in pair:
            copy.start()
        copies.append(pair)

    for copy in index_copies:
        copy.wait()
    square = (LANES, LANES)
    cluster = cluster_ref[...]
    high, low = cluster >> 7, cluster & 127
    by_low = dot(owner_ref[...].astype(F32).astype(BF16), hot(iota(square, 0) == low))
    owner = jnp.sum(jnp.where(iota(by_low.shape, 0) == high, by_low, 0.0), axis=0, keepdims=True)
    owner = owner.astype(jnp.int32)
    owner_hot = hot(iota(square, 0) == owner)
    same = lax.dot_general(
        owner_hot, owner_hot, (((0,), (0,)), ((), ())), preferred_element_type=F32
    )
    slot = jnp.sum(jnp.where(iota(square, 0) < iota(square, 1), same, 0.0), axis=0, keepdims=True)
    target = owner * SLOTS + slot.astype(jnp.int32)
    target_ref[...] = jnp.broadcast_to(target, target_ref.shape)

    live = live_ref[...] == 1
    high_label = jnp.where(live, high + 1, 0)
    low_label = jnp.where(live, low, 0)
    line = iota(square, 0)
    part = jnp.where((line & 7) == 0, high_label, jnp.where((line & 7) == 1, low_label, 0))
    part = jnp.where((line >> 3) == (target >> 4), part, 0).astype(F32).astype(BF16)
    labels = dot_nt(part, hot(line == (target & 15))).reshape(PLANES, 8, LANES)
    hit = hot(iota((SLAB, LANES), 0) == target)

    projected = jnp.zeros(prefix_ref.shape, F32)
    for part, pair in enumerate(copies):
        for copy in pair:
            copy.wait()
        projected += dot(embeds_buf[part], head_buf[part])
    norm = lax.rsqrt(jnp.sum(projected * projected, axis=1, keepdims=True) + NORM_EPS)
    prefix = (projected * norm).astype(BF16)
    prefix_ref[...] = prefix
    rows = dot(hit, prefix).reshape(PLANES, PLANE_SLOTS, 2 * LANES)
    send_ref[...] = jnp.concatenate(
        [rows[:, :, :LANES], rows[:, :, LANES:], labels], axis=1
    ).astype(BF16)


def sort_kernel(got_ref, send_ref):
    got = got_ref[...].astype(F32)
    low = got[:, :PLANE_SLOTS].reshape(SLAB, LANES).astype(BF16)
    high = got[:, PLANE_SLOTS : 2 * PLANE_SLOTS].reshape(SLAB, LANES).astype(BF16)
    dest = iota((SLAB, SLAB), 0)
    source = ((dest >> 1) & 15) * PLANE_SLOTS + (dest >> 5) * SLOTS + (dest & 1)
    order = hot(iota((SLAB, SLAB), 1) == source)
    rows = dot(order, jnp.concatenate([low, high], axis=1))
    rows = rows.reshape(COLUMNS, OWNER_SLOTS, 2 * LANES)

    square = (LANES, LANES)
    tiles = got[:, 2 * PLANE_SLOTS :].reshape(PLANES * 8, LANES).astype(BF16)
    line, lane = iota(square, 0), iota(square, 1)
    pick = ((line & 31) >> 1) * 8 + (line >> 5)
    spread = dot(hot((lane == pick) & (line < 2 * OWNER_SLOTS)), tiles)
    spread = jnp.where((lane & 1) == (line & 1), spread, 0.0).astype(BF16)
    group = (COLUMNS * 8, LANES)
    labels = dot_nt(hot((iota(group, 1) >> 1) == (iota(group, 0) >> 3)), spread)
    labels = labels.reshape(COLUMNS, 8, LANES)
    out = jnp.concatenate([rows[:, :, :LANES], rows[:, :, LANES:], labels], axis=1).astype(BF16)
    for helper in range(HELPERS):
        send_ref[:, helper] = out


def best_kernel(got_ref, out_ref):
    helper = lax.axis_index("help")
    sources = COLUMNS * HELPERS
    total = sources * OWNER_SLOTS
    low = got_ref[:, :, :OWNER_SLOTS].reshape(total, LANES)
    high = got_ref[:, :, OWNER_SLOTS : 2 * OWNER_SLOTS].reshape(total, LANES)
    columns = jnp.concatenate([low, high], axis=1)
    own_low = got_ref[:, helper, :OWNER_SLOTS].reshape(SLAB, LANES)
    own_high = got_ref[:, helper, OWNER_SLOTS : 2 * OWNER_SLOTS].reshape(SLAB, LANES)

    dest = iota((SLAB, SLAB), 0)
    in_owner = ((dest >> 3) & 15) * SLOTS + (dest >> 7)
    order = hot(iota((SLAB, SLAB), 1) == (dest & 7) * OWNER_SLOTS + in_owner)
    own = dot(order, jnp.concatenate([own_low, own_high], axis=1)).astype(BF16)
    scores = dot_nt(own, columns)

    tiles = got_ref[...].astype(F32)[:, :, 2 * OWNER_SLOTS :].reshape(sources * 8, LANES).astype(BF16)
    shape = (total, sources * 8)
    spread = dot(hot(iota(shape, 1) == (iota(shape, 0) >> 5) * 8), tiles)
    line, lane = iota((total, LANES), 0) & 31, iota((total, LANES), 1)
    spread = jnp.where(lane == line, spread * 128.0, jnp.where(lane == line + 32, spread, 0.0))
    column_label = dot_nt(jnp.ones((8, LANES), BF16), spread.astype(BF16))[:1]

    shape = (SLAB, sources * 8)
    line = iota(shape, 0)
    own_spread = dot(hot(iota(shape, 1) == ((line & 7) * HELPERS + helper) * 8), tiles)
    line, lane = iota((SLAB, LANES), 0), iota((SLAB, LANES), 1)
    line = ((line >> 3) & 15) * SLOTS + (line >> 7)
    own_label = jnp.sum(
        jnp.where(lane == line, own_spread * 128.0, jnp.where(lane == line + 32, own_spread, 0.0)),
        axis=1,
        keepdims=True,
    )
    own_label = jnp.where(own_label > 0.5, own_label, -1.0)
    line = iota((SLAB, 1), 0)
    own_index = ((line & 7) * HELPERS + helper) * OWNER_SLOTS + ((line >> 3) & 15) * SLOTS + (line >> 7)
    allowed = (own_label == column_label) & (own_index != iota((SLAB, total), 1))
    best = jnp.max(jnp.where(allowed, scores, -1.0), axis=1, keepdims=True)
    half = SLAB // 2
    lane = iota(out_ref.shape, 1)
    out_ref[...] = jnp.where(lane == 0, best[:half], jnp.where(lane == 1, best[half:], 0.0))


def finish_kernel(got_ref, target_ref, live_ref, out_ref):
    got = got_ref[...]
    target = target_ref[:1]
    value = jnp.where((target & 1) == 0, got[:, 0:1], got[:, 1:2])
    value = jnp.where(iota(got.shape, 0) == (target >> 1), value, 0.0)
    value = jnp.sum(value, axis=0, keepdims=True)
    out_ref[...] = jnp.where(live_ref[...] == 1, value, -1.0)


VMEM = pl.BlockSpec(memory_space=pltpu.VMEM)
ANY = pl.BlockSpec(memory_space=pl.ANY)
LIMIT = pltpu.CompilerParams(vmem_limit_bytes=32 * 1024 * 1024)


def shards(embeds, head_rows, cluster_of, owner_of, live_mask):
    row_count, width = embeds.shape
    depth = width // CHUNKS
    live = live_mask.reshape(1, row_count)
    prefix, send, target = pl.pallas_call(
        project_kernel,
        out_shape=(
            jax.ShapeDtypeStruct((row_count, 2 * LANES), BF16),
            jax.ShapeDtypeStruct((PLANES, 2 * PLANE_SLOTS + 8, LANES), BF16),
            jax.ShapeDtypeStruct((8, row_count), jnp.int32),
        ),
        in_specs=[ANY] * 5,
        out_specs=(VMEM, VMEM, VMEM),
        scratch_shapes=[
            pltpu.VMEM((CHUNKS, row_count, depth), BF16),
            pltpu.VMEM((CHUNKS, depth, 2 * LANES), BF16),
            pltpu.VMEM((1, row_count), jnp.int32),
            pltpu.VMEM((owner_of.shape[0] // LANES, LANES), jnp.int32),
            pltpu.VMEM((1, row_count), jnp.int32),
            pltpu.SemaphoreType.DMA((CHUNKS,)),
            pltpu.SemaphoreType.DMA((CHUNKS,)),
            pltpu.SemaphoreType.DMA((3,)),
        ],
        compiler_params=pltpu.CompilerParams(vmem_limit_bytes=60 * 1024 * 1024),
        name="project",
    )(embeds, head_rows, cluster_of.reshape(1, row_count), owner_of.reshape(-1, LANES), live)
    got = lax.all_to_all(send, "z", split_axis=0, concat_axis=0, tiled=True)
    lines = 2 * OWNER_SLOTS + 8
    send = pl.pallas_call(
        sort_kernel,
        out_shape=jax.ShapeDtypeStruct((COLUMNS, HELPERS, lines, LANES), BF16),
        in_specs=[VMEM],
        out_specs=VMEM,
        compiler_params=LIMIT,
        name="sort",
    )(got)
    got = lax.all_to_all(
        send.reshape(COLUMNS * HELPERS, lines, LANES),
        ("x", "core", "help"),
        split_axis=0,
        concat_axis=0,
        tiled=True,
    )
    best = pl.pallas_call(
        best_kernel,
        out_shape=jax.ShapeDtypeStruct((PLANES * COLUMNS, LANES), F32),
        in_specs=[VMEM],
        out_specs=VMEM,
        compiler_params=LIMIT,
        name="best",
    )(got.reshape(COLUMNS, HELPERS, lines, LANES))
    back = lax.all_to_all(best, ("z", "x", "core"), split_axis=0, concat_axis=0, tiled=True)
    nearest = pl.pallas_call(
        finish_kernel,
        out_shape=jax.ShapeDtypeStruct((1, row_count), F32),
        in_specs=[VMEM, VMEM, VMEM],
        out_specs=VMEM,
        compiler_params=LIMIT,
        name="finish",
    )(back, target, live)
    return (prefix, nearest.reshape(row_count))


def solution(mesh):
    axes = ("z", "x", "core", "help")
    fine = Mesh(mesh.devices.reshape(PLANES, 4, 2, HELPERS), axes)
    return jax.shard_map(
        shards,
        mesh=fine,
        in_specs=(P(axes, None), P(), P(axes), P(), P(axes)),
        out_specs=(P(axes, None), P(axes)),
        check_vma=False,
    )
```

```python
import functools

import jax
import jax.numpy as jnp
from jax import lax
from jax.experimental import pallas as pl
from jax.experimental.pallas import tpu as pltpu
from jax.sharding import Mesh, PartitionSpec as P

NORM_EPS = 1e-06
LANES = 128
PLANES = 16
COLUMNS = 8
HELPERS = 4
SLOTS = 2
PLANE_SLOTS = COLUMNS * SLOTS
SLAB = PLANES * PLANE_SLOTS
OWNER_SLOTS = PLANES * SLOTS
CHUNKS = 4
PLANE_TURN = 8
COLUMN_TURN = 4

F32 = jnp.float32
BF16 = jnp.bfloat16


def iota(shape, dim):
    return lax.broadcasted_iota(jnp.int32, shape, dim)


def hot(condition):
    return jnp.where(condition, 1.0, 0.0).astype(BF16)


def dot_nt(left, right):
    return lax.dot_general(left, right, (((1,), (1,)), ((), ())), preferred_element_type=F32)


def dot(left, right):
    return jnp.dot(left, right, preferred_element_type=F32)


def project_kernel(
    embeds, head, cluster, owner_of, live_mask, prefix_ref, send_ref, target_ref,
    embeds_buf, head_buf, cluster_ref, owner_ref, live_ref, embeds_sem, head_sem, index_sem,
):
    depth = head_buf.shape[1]
    index_copies = [
        pltpu.make_async_copy(source, buf, index_sem.at[spot])
        for spot, (source, buf) in enumerate(
            ((cluster, cluster_ref), (owner_of, owner_ref), (live_mask, live_ref))
        )
    ]
    for copy in index_copies:
        copy.start()
    copies = []
    for part in range(CHUNKS):
        span = pl.ds(part * depth, depth)
        pair = (
            pltpu.make_async_copy(head.at[span, :], head_buf.at[part], head_sem.at[part]),
            pltpu.make_async_copy(embeds.at[:, span], embeds_buf.at[part], embeds_sem.at[part]),
        )
        for copy in pair:
            copy.start()
        copies.append(pair)

    for copy in index_copies:
        copy.wait()
    square = (LANES, LANES)
    cluster = cluster_ref[...]
    high, low = cluster >> 7, cluster & 127
    by_low = dot(owner_ref[...].astype(F32).astype(BF16), hot(iota(square, 0) == low))
    owner = jnp.sum(jnp.where(iota(by_low.shape, 0) == high, by_low, 0.0), axis=0, keepdims=True)
    owner = owner.astype(jnp.int32)
    owner_hot = hot(iota(square, 0) == owner)
    same = lax.dot_general(
        owner_hot, owner_hot, (((0,), (0,)), ((), ())), preferred_element_type=F32
    )
    slot = jnp.sum(jnp.where(iota(square, 0) < iota(square, 1), same, 0.0), axis=0, keepdims=True)
    target = owner * SLOTS + slot.astype(jnp.int32)
    target = target ^ (PLANE_TURN * PLANE_SLOTS)
    target_ref[...] = jnp.broadcast_to(target ^ (COLUMN_TURN * SLOTS), target_ref.shape)

    live = live_ref[...] == 1
    high_label = jnp.where(live, high + 1, 0)
    low_label = jnp.where(live, low, 0)
    line = iota(square, 0)
    part = jnp.where((line & 7) == 0, high_label, jnp.where((line & 7) == 1, low_label, 0))
    part = jnp.where((line >> 3) == (target >> 4), part, 0).astype(F32).astype(BF16)
    labels = dot_nt(part, hot(line == (target & 15))).reshape(PLANES, 8, LANES)
    hit = hot(iota((SLAB, LANES), 0) == target)

    projected = jnp.zeros(prefix_ref.shape, F32)
    for part, pair in enumerate(copies):
        for copy in pair:
            copy.wait()
        projected += dot(embeds_buf[part], head_buf[part])
    norm = lax.rsqrt(jnp.sum(projected * projected, axis=1, keepdims=True) + NORM_EPS)
    prefix = (projected * norm).astype(BF16)
    prefix_ref[...] = prefix
    rows = dot(hit, prefix).reshape(PLANES, PLANE_SLOTS, 2 * LANES)
    send_ref[...] = jnp.concatenate(
        [rows[:, :, :LANES], rows[:, :, LANES:], labels], axis=1
    ).astype(BF16)


def sort_kernel(got_ref, send_ref):
    got = got_ref[...].astype(F32)
    low = got[:, :PLANE_SLOTS].reshape(SLAB, LANES).astype(BF16)
    high = got[:, PLANE_SLOTS : 2 * PLANE_SLOTS].reshape(SLAB, LANES).astype(BF16)
    dest = iota((SLAB, SLAB), 0)
    source = ((dest >> 1) & 15) * PLANE_SLOTS + (dest >> 5) * SLOTS + (dest & 1)
    order = hot(iota((SLAB, SLAB), 1) == source)
    rows = dot(order, jnp.concatenate([low, high], axis=1))
    rows = rows.reshape(COLUMNS, OWNER_SLOTS, 2 * LANES)

    square = (LANES, LANES)
    tiles = got[:, 2 * PLANE_SLOTS :].reshape(PLANES * 8, LANES).astype(BF16)
    line, lane = iota(square, 0), iota(square, 1)
    pick = ((line & 31) >> 1) * 8 + (line >> 5)
    spread = dot(hot((lane == pick) & (line < 2 * OWNER_SLOTS)), tiles)
    spread = jnp.where((lane & 1) == (line & 1), spread, 0.0).astype(BF16)
    group = (COLUMNS * 8, LANES)
    labels = dot_nt(hot((iota(group, 1) >> 1) == (iota(group, 0) >> 3)), spread)
    labels = labels.reshape(COLUMNS, 8, LANES)
    out = jnp.concatenate([rows[:, :, :LANES], rows[:, :, LANES:], labels], axis=1).astype(BF16)
    for helper in range(HELPERS):
        send_ref[:, helper] = out


def best_kernel(got_ref, out_ref):
    helper = lax.axis_index("help")
    sources = COLUMNS * HELPERS
    total = sources * OWNER_SLOTS
    low = got_ref[:, :, :OWNER_SLOTS].reshape(total, LANES)
    high = got_ref[:, :, OWNER_SLOTS : 2 * OWNER_SLOTS].reshape(total, LANES)
    columns = jnp.concatenate([low, high], axis=1)
    own_low = got_ref[:, helper, :OWNER_SLOTS].reshape(SLAB, LANES)
    own_high = got_ref[:, helper, OWNER_SLOTS : 2 * OWNER_SLOTS].reshape(SLAB, LANES)

    dest = iota((SLAB, SLAB), 0)
    in_owner = ((dest >> 3) & 15) * SLOTS + (dest >> 7)
    order = hot(iota((SLAB, SLAB), 1) == ((dest & 7) ^ COLUMN_TURN) * OWNER_SLOTS + in_owner)
    own = dot(order, jnp.concatenate([own_low, own_high], axis=1)).astype(BF16)
    scores = dot_nt(own, columns)

    tiles = got_ref[...].astype(F32)[:, :, 2 * OWNER_SLOTS :].reshape(sources * 8, LANES).astype(BF16)
    shape = (total, sources * 8)
    spread = dot(hot(iota(shape, 1) == (iota(shape, 0) >> 5) * 8), tiles)
    line, lane = iota((total, LANES), 0) & 31, iota((total, LANES), 1)
    spread = jnp.where(lane == line, spread * 128.0, jnp.where(lane == line + 32, spread, 0.0))
    column_label = dot_nt(jnp.ones((8, LANES), BF16), spread.astype(BF16))[:1]

    shape = (SLAB, sources * 8)
    line = iota(shape, 0)
    own_spread = dot(hot(iota(shape, 1) == (((line & 7) ^ COLUMN_TURN) * HELPERS + helper) * 8), tiles)
    line, lane = iota((SLAB, LANES), 0), iota((SLAB, LANES), 1)
    line = ((line >> 3) & 15) * SLOTS + (line >> 7)
    own_label = jnp.sum(
        jnp.where(lane == line, own_spread * 128.0, jnp.where(lane == line + 32, own_spread, 0.0)),
        axis=1,
        keepdims=True,
    )
    own_label = jnp.where(own_label > 0.5, own_label, -1.0)
    line = iota((SLAB, 1), 0)
    own_index = (((line & 7) ^ COLUMN_TURN) * HELPERS + helper) * OWNER_SLOTS + ((line >> 3) & 15) * SLOTS + (line >> 7)
    allowed = (own_label == column_label) & (own_index != iota((SLAB, total), 1))
    best = jnp.max(jnp.where(allowed, scores, -1.0), axis=1, keepdims=True)
    half = SLAB // 2
    lane = iota(out_ref.shape, 1)
    out_ref[...] = jnp.where(lane == 0, best[:half], jnp.where(lane == 1, best[half:], 0.0))


def finish_kernel(got_ref, target_ref, live_ref, out_ref):
    got = got_ref[...]
    target = target_ref[:1]
    value = jnp.where((target & 1) == 0, got[:, 0:1], got[:, 1:2])
    value = jnp.where(iota(got.shape, 0) == (target >> 1), value, 0.0)
    value = jnp.sum(value, axis=0, keepdims=True)
    out_ref[...] = jnp.where(live_ref[...] == 1, value, -1.0)


VMEM = pl.BlockSpec(memory_space=pltpu.VMEM)
ANY = pl.BlockSpec(memory_space=pl.ANY)
LIMIT = pltpu.CompilerParams(vmem_limit_bytes=32 * 1024 * 1024)


def shards(embeds, head_rows, cluster_of, owner_of, live_mask):
    row_count, width = embeds.shape
    depth = width // CHUNKS
    live = live_mask.reshape(1, row_count)
    prefix, send, target = pl.pallas_call(
        project_kernel,
        out_shape=(
            jax.ShapeDtypeStruct((row_count, 2 * LANES), BF16),
            jax.ShapeDtypeStruct((PLANES, 2 * PLANE_SLOTS + 8, LANES), BF16),
            jax.ShapeDtypeStruct((8, row_count), jnp.int32),
        ),
        in_specs=[ANY] * 5,
        out_specs=(VMEM, VMEM, VMEM),
        scratch_shapes=[
            pltpu.VMEM((CHUNKS, row_count, depth), BF16),
            pltpu.VMEM((CHUNKS, depth, 2 * LANES), BF16),
            pltpu.VMEM((1, row_count), jnp.int32),
            pltpu.VMEM((owner_of.shape[0] // LANES, LANES), jnp.int32),
            pltpu.VMEM((1, row_count), jnp.int32),
            pltpu.SemaphoreType.DMA((CHUNKS,)),
            pltpu.SemaphoreType.DMA((CHUNKS,)),
            pltpu.SemaphoreType.DMA((3,)),
        ],
        compiler_params=pltpu.CompilerParams(vmem_limit_bytes=60 * 1024 * 1024),
        name="project",
    )(embeds, head_rows, cluster_of.reshape(1, row_count), owner_of.reshape(-1, LANES), live)
    planes = [[spot ^ PLANE_TURN for spot in range(PLANES)]]
    got = lax.all_to_all(
        send, "z", split_axis=0, concat_axis=0, tiled=True, axis_index_groups=planes
    )
    lines = 2 * OWNER_SLOTS + 8
    send = pl.pallas_call(
        sort_kernel,
        out_shape=jax.ShapeDtypeStruct((COLUMNS, HELPERS, lines, LANES), BF16),
        in_specs=[VMEM],
        out_specs=VMEM,
        compiler_params=LIMIT,
        name="sort",
    )(got)
    got = lax.all_to_all(
        send.reshape(COLUMNS * HELPERS, lines, LANES),
        ("x", "core", "help"),
        split_axis=0,
        concat_axis=0,
        tiled=True,
    )
    best = pl.pallas_call(
        best_kernel,
        out_shape=jax.ShapeDtypeStruct((PLANES * COLUMNS, LANES), F32),
        in_specs=[VMEM],
        out_specs=VMEM,
        compiler_params=LIMIT,
        name="best",
    )(got.reshape(COLUMNS, HELPERS, lines, LANES))
    turn = PLANE_TURN * COLUMNS + COLUMN_TURN
    owners = [[spot ^ turn for spot in range(PLANES * COLUMNS)]]
    back = lax.all_to_all(
        best, ("z", "x", "core"), split_axis=0, concat_axis=0, tiled=True, axis_index_groups=owners
    )
    nearest = pl.pallas_call(
        finish_kernel,
        out_shape=jax.ShapeDtypeStruct((1, row_count), F32),
        in_specs=[VMEM, VMEM, VMEM],
        out_specs=VMEM,
        compiler_params=LIMIT,
        name="finish",
    )(back, target, live)
    return (prefix, nearest.reshape(row_count))


def solution(mesh):
    axes = ("z", "x", "core", "help")
    fine = Mesh(mesh.devices.reshape(PLANES, 4, 2, HELPERS), axes)
    return jax.shard_map(
        shards,
        mesh=fine,
        in_specs=(P(axes, None), P(), P(axes), P(), P(axes)),
        out_specs=(P(axes, None), P(axes)),
        check_vma=False,
    )
```

```python
import jax
import jax.numpy as jnp
from jax import lax
from jax.experimental import pallas as pl
from jax.experimental.pallas import tpu as pltpu
from jax.sharding import Mesh, PartitionSpec as P

NORM_EPS = 1e-06
LANES = 128
PLANES = 16
COLUMNS = 8
HELPERS = 4
SLOTS = 2
PLANE_SLOTS = COLUMNS * SLOTS
SLAB = PLANES * PLANE_SLOTS
OWNER_SLOTS = PLANES * SLOTS
PIECES = 2 * PLANE_SLOTS // 8
PLANE_TURN = 8
COLUMN_TURN = 4

F32 = jnp.float32
BF16 = jnp.bfloat16


def iota(shape, dim):
    return lax.broadcasted_iota(jnp.int32, shape, dim)


def hot(condition):
    return jnp.where(condition, 1.0, 0.0).astype(BF16)


def dot_nt(left, right):
    return lax.dot_general(left, right, (((1,), (1,)), ((), ())), preferred_element_type=F32)


def dot(left, right):
    return jnp.dot(left, right, preferred_element_type=F32)


def scatter_kernel(prefix_ref, cluster_ref, owner_ref, live_ref, send_ref, target_ref):
    square = (LANES, LANES)
    cluster = cluster_ref[...]
    high, low = cluster >> 7, cluster & 127
    by_low = dot(owner_ref[...].astype(F32).astype(BF16), hot(iota(square, 0) == low))
    owner = jnp.sum(jnp.where(iota(by_low.shape, 0) == high, by_low, 0.0), axis=0, keepdims=True)
    owner = owner.astype(jnp.int32)
    owner_hot = hot(iota(square, 0) == owner)
    same = lax.dot_general(
        owner_hot, owner_hot, (((0,), (0,)), ((), ())), preferred_element_type=F32
    )
    slot = jnp.sum(jnp.where(iota(square, 0) < iota(square, 1), same, 0.0), axis=0, keepdims=True)
    target = owner * SLOTS + slot.astype(jnp.int32)
    target = target ^ (PLANE_TURN * PLANE_SLOTS)
    target_ref[...] = jnp.broadcast_to(target ^ (COLUMN_TURN * SLOTS), target_ref.shape)

    live = live_ref[...] == 1
    high_label = jnp.where(live, high + 1, 0)
    low_label = jnp.where(live, low, 0)
    line = iota(square, 0)
    part = jnp.where((line & 7) == 0, high_label, jnp.where((line & 7) == 1, low_label, 0))
    part = jnp.where((line >> 3) == (target >> 4), part, 0).astype(F32).astype(BF16)
    labels = dot_nt(part, hot(line == (target & 15))).reshape(PLANES, 8, LANES)

    rows = dot(hot(iota((SLAB, LANES), 0) == target), prefix_ref[...])
    rows = rows.reshape(PLANES, PLANE_SLOTS, 2 * LANES)
    rows = jnp.concatenate([rows[:, :, :LANES], rows[:, :, LANES:]], axis=1)
    rows = rows.reshape(PLANES, PIECES, 8, LANES)
    send_ref[...] = jnp.concatenate(
        [rows[:, :, :4], rows[:, :, 4:], labels[:, :4].reshape(PLANES, 1, 4, LANES)], axis=1
    ).astype(BF16)


def sort_kernel(got_ref, send_ref):
    pieces = got_ref[...].astype(F32)
    got = jnp.concatenate([pieces[:, :PIECES], pieces[:, PIECES : 2 * PIECES]], axis=2)
    got = got.reshape(PLANES, 2 * PLANE_SLOTS, LANES)
    low = got[:, :PLANE_SLOTS].reshape(SLAB, LANES).astype(BF16)
    high = got[:, PLANE_SLOTS:].reshape(SLAB, LANES).astype(BF16)
    dest = iota((SLAB, SLAB), 0)
    source = ((dest >> 1) & 15) * PLANE_SLOTS + (dest >> 5) * SLOTS + (dest & 1)
    order = hot(iota((SLAB, SLAB), 1) == source)
    rows = dot(order, jnp.concatenate([low, high], axis=1))
    rows = rows.reshape(COLUMNS, OWNER_SLOTS, 2 * LANES)

    square = (LANES, LANES)
    tiles = pieces[:, 2 * PIECES].reshape(PLANES, 4, LANES)
    tiles = jnp.concatenate([tiles, tiles], axis=1).reshape(PLANES * 8, LANES).astype(BF16)
    line, lane = iota(square, 0), iota(square, 1)
    pick = ((line & 31) >> 1) * 8 + (line >> 5)
    spread = dot(hot((lane == pick) & (line < 2 * OWNER_SLOTS)), tiles)
    spread = jnp.where((lane & 1) == (line & 1), spread, 0.0).astype(BF16)
    group = (COLUMNS * 8, LANES)
    labels = dot_nt(hot((iota(group, 1) >> 1) == (iota(group, 0) >> 3)), spread)
    labels = labels.reshape(COLUMNS, 8, LANES)
    out = jnp.concatenate([rows[:, :, :LANES], rows[:, :, LANES:], labels], axis=1).astype(BF16)
    for helper in range(HELPERS):
        send_ref[:, helper] = out


def best_kernel(got_ref, out_ref):
    helper = lax.axis_index("help")
    sources = COLUMNS * HELPERS
    total = sources * OWNER_SLOTS
    low = got_ref[:, :, :OWNER_SLOTS].reshape(total, LANES)
    high = got_ref[:, :, OWNER_SLOTS : 2 * OWNER_SLOTS].reshape(total, LANES)
    columns = jnp.concatenate([low, high], axis=1)
    own_low = got_ref[:, helper, :OWNER_SLOTS].reshape(SLAB, LANES)
    own_high = got_ref[:, helper, OWNER_SLOTS : 2 * OWNER_SLOTS].reshape(SLAB, LANES)

    dest = iota((SLAB, SLAB), 0)
    in_owner = ((dest >> 3) & 15) * SLOTS + (dest >> 7)
    order = hot(iota((SLAB, SLAB), 1) == ((dest & 7) ^ COLUMN_TURN) * OWNER_SLOTS + in_owner)
    own = dot(order, jnp.concatenate([own_low, own_high], axis=1)).astype(BF16)
    scores = dot_nt(own, columns)

    tiles = got_ref[...].astype(F32)[:, :, 2 * OWNER_SLOTS :].reshape(sources * 8, LANES).astype(BF16)
    shape = (total, sources * 8)
    spread = dot(hot(iota(shape, 1) == (iota(shape, 0) >> 5) * 8), tiles)
    line, lane = iota((total, LANES), 0) & 31, iota((total, LANES), 1)
    spread = jnp.where(lane == line, spread * 128.0, jnp.where(lane == line + 32, spread, 0.0))
    column_label = dot_nt(jnp.ones((8, LANES), BF16), spread.astype(BF16))[:1]

    shape = (SLAB, sources * 8)
    line = iota(shape, 0)
    own_spread = dot(hot(iota(shape, 1) == (((line & 7) ^ COLUMN_TURN) * HELPERS + helper) * 8), tiles)
    line, lane = iota((SLAB, LANES), 0), iota((SLAB, LANES), 1)
    line = ((line >> 3) & 15) * SLOTS + (line >> 7)
    own_label = jnp.sum(
        jnp.where(lane == line, own_spread * 128.0, jnp.where(lane == line + 32, own_spread, 0.0)),
        axis=1,
        keepdims=True,
    )
    own_label = jnp.where(own_label > 0.5, own_label, -1.0)
    line = iota((SLAB, 1), 0)
    own_index = (((line & 7) ^ COLUMN_TURN) * HELPERS + helper) * OWNER_SLOTS + ((line >> 3) & 15) * SLOTS + (line >> 7)
    allowed = (own_label == column_label) & (own_index != iota((SLAB, total), 1))
    best = jnp.max(jnp.where(allowed, scores, -1.0), axis=1, keepdims=True)
    half = SLAB // 2
    lane = iota(out_ref.shape, 1)
    out_ref[...] = jnp.where(lane == 0, best[:half], jnp.where(lane == 1, best[half:], 0.0))


def finish_kernel(got_ref, target_ref, live_ref, out_ref):
    got = got_ref[...]
    target = target_ref[:1]
    value = jnp.where((target & 1) == 0, got[:, 0:1], got[:, 1:2])
    value = jnp.where(iota(got.shape, 0) == (target >> 1), value, 0.0)
    value = jnp.sum(value, axis=0, keepdims=True)
    out_ref[...] = jnp.where(live_ref[...] == 1, value, -1.0)


VMEM = pl.BlockSpec(memory_space=pltpu.VMEM)
LIMIT = pltpu.CompilerParams(vmem_limit_bytes=32 * 1024 * 1024)


def shards(embeds, head_rows, cluster_of, owner_of, live_mask):
    row_count = embeds.shape[0]
    live = live_mask.reshape(1, row_count)
    projected = jnp.dot(embeds, head_rows, preferred_element_type=F32)
    norm = lax.rsqrt(jnp.sum(projected * projected, axis=1, keepdims=True) + NORM_EPS)
    prefix = (projected * norm).astype(BF16)
    send, target = pl.pallas_call(
        scatter_kernel,
        out_shape=(
            jax.ShapeDtypeStruct((PLANES, 2 * PIECES + 1, 4, LANES), BF16),
            jax.ShapeDtypeStruct((8, row_count), jnp.int32),
        ),
        in_specs=[VMEM] * 4,
        out_specs=(VMEM, VMEM),
        compiler_params=LIMIT,
        name="scatter",
    )(prefix, cluster_of.reshape(1, row_count), owner_of.reshape(-1, LANES), live)
    planes = [[spot ^ PLANE_TURN for spot in range(PLANES)]]
    got = lax.all_to_all(
        send, "z", split_axis=0, concat_axis=0, tiled=True, axis_index_groups=planes
    )
    lines = 2 * OWNER_SLOTS + 8
    send = pl.pallas_call(
        sort_kernel,
        out_shape=jax.ShapeDtypeStruct((COLUMNS, HELPERS, lines, LANES), BF16),
        in_specs=[VMEM],
        out_specs=VMEM,
        compiler_params=LIMIT,
        name="sort",
    )(got)
    got = lax.all_to_all(
        send.reshape(COLUMNS * HELPERS, lines, LANES),
        ("x", "core", "help"),
        split_axis=0,
        concat_axis=0,
        tiled=True,
    )
    best = pl.pallas_call(
        best_kernel,
        out_shape=jax.ShapeDtypeStruct((PLANES * COLUMNS, LANES), F32),
        in_specs=[VMEM],
        out_specs=VMEM,
        compiler_params=LIMIT,
        name="best",
    )(got.reshape(COLUMNS, HELPERS, lines, LANES))
    turn = PLANE_TURN * COLUMNS + COLUMN_TURN
    owners = [[spot ^ turn for spot in range(PLANES * COLUMNS)]]
    back = lax.all_to_all(
        best, ("z", "x", "core"), split_axis=0, concat_axis=0, tiled=True, axis_index_groups=owners
    )
    nearest = pl.pallas_call(
        finish_kernel,
        out_shape=jax.ShapeDtypeStruct((1, row_count), F32),
        in_specs=[VMEM, VMEM, VMEM],
        out_specs=VMEM,
        compiler_params=LIMIT,
        name="finish",
    )(back, target, live)
    return (prefix, nearest.reshape(row_count))


def solution(mesh):
    axes = ("z", "x", "core", "help")
    fine = Mesh(mesh.devices.reshape(PLANES, 4, 2, HELPERS), axes)
    return jax.shard_map(
        shards,
        mesh=fine,
        in_specs=(P(axes, None), P(), P(axes), P(), P(axes)),
        out_specs=(P(axes, None), P(axes)),
        check_vma=False,
    )
```

```python
import jax
import jax.numpy as jnp
from jax import lax
from jax.experimental import pallas as pl
from jax.experimental.pallas import tpu as pltpu
from jax.sharding import Mesh, PartitionSpec as P

NORM_EPS = 1e-06
LANES = 128
PLANES = 16
COLUMNS = 8
HELPERS = 4
SLOTS = 2
PLANE_SLOTS = COLUMNS * SLOTS
SLAB = PLANES * PLANE_SLOTS
OWNER_SLOTS = PLANES * SLOTS
PIECES = 2 * PLANE_SLOTS // 8
PLANE_TURN = 8
COLUMN_TURN = 4

F32 = jnp.float32
BF16 = jnp.bfloat16


def iota(shape, dim):
    return lax.broadcasted_iota(jnp.int32, shape, dim)


def hot(condition):
    return jnp.where(condition, 1.0, 0.0).astype(BF16)


def dot_nt(left, right):
    return lax.dot_general(left, right, (((1,), (1,)), ((), ())), preferred_element_type=F32)


def dot(left, right):
    return jnp.dot(left, right, preferred_element_type=F32)


def index_kernel(packed_ref, target_ref, hit_ref, label_ref):
    square = (LANES, LANES)
    cluster = packed_ref[16:17]
    high, low = cluster >> 7, cluster & 127
    by_low = dot(packed_ref[:16].astype(F32).astype(BF16), hot(iota(square, 0) == low))
    owner = jnp.sum(jnp.where(iota(by_low.shape, 0) == high, by_low, 0.0), axis=0, keepdims=True)
    owner = owner.astype(jnp.int32)
    owner_hot = hot(iota(square, 0) == owner)
    same = lax.dot_general(
        owner_hot, owner_hot, (((0,), (0,)), ((), ())), preferred_element_type=F32
    )
    slot = jnp.sum(jnp.where(iota(square, 0) < iota(square, 1), same, 0.0), axis=0, keepdims=True)
    target = owner * SLOTS + slot.astype(jnp.int32)
    target = target ^ (PLANE_TURN * PLANE_SLOTS)
    target_ref[...] = jnp.broadcast_to(target ^ (COLUMN_TURN * SLOTS), target_ref.shape)

    live = packed_ref[17:18] == 1
    high_label = jnp.where(live, high + 1, 0)
    low_label = jnp.where(live, low, 0)
    line = iota(square, 0)
    part = jnp.where((line & 7) == 0, high_label, jnp.where((line & 7) == 1, low_label, 0))
    part = jnp.where((line >> 3) == (target >> 4), part, 0).astype(F32).astype(BF16)
    label_ref[...] = dot_nt(part, hot(line == (target & 15)))
    hit_ref[...] = hot(iota((SLAB, LANES), 0) == target)


def scatter_kernel(prefix_ref, hit_ref, label_ref, send_ref):
    rows = dot(hit_ref[...], prefix_ref[...]).reshape(PLANES, PLANE_SLOTS, 2 * LANES)
    rows = jnp.concatenate([rows[:, :, :LANES], rows[:, :, LANES:]], axis=1)
    rows = rows.reshape(PLANES, PIECES, 8, LANES)
    labels = label_ref[...].reshape(PLANES, 1, 8, LANES)
    send_ref[...] = jnp.concatenate(
        [rows[:, :, :4], rows[:, :, 4:], labels[:, :, :4]], axis=1
    ).astype(BF16)


def sort_kernel(got_ref, send_ref):
    pieces = got_ref[...].astype(F32)
    got = jnp.concatenate([pieces[:, :PIECES], pieces[:, PIECES : 2 * PIECES]], axis=2)
    got = got.reshape(PLANES, 2 * PLANE_SLOTS, LANES)
    low = got[:, :PLANE_SLOTS].reshape(SLAB, LANES).astype(BF16)
    high = got[:, PLANE_SLOTS:].reshape(SLAB, LANES).astype(BF16)
    dest = iota((SLAB, SLAB), 0)
    source = ((dest >> 1) & 15) * PLANE_SLOTS + (dest >> 5) * SLOTS + (dest & 1)
    order = hot(iota((SLAB, SLAB), 1) == source)
    rows = dot(order, jnp.concatenate([low, high], axis=1))
    rows = rows.reshape(COLUMNS, OWNER_SLOTS, 2 * LANES)

    square = (LANES, LANES)
    tiles = pieces[:, 2 * PIECES].reshape(PLANES, 4, LANES)
    tiles = jnp.concatenate([tiles, tiles], axis=1).reshape(PLANES * 8, LANES).astype(BF16)
    line, lane = iota(square, 0), iota(square, 1)
    pick = ((line & 31) >> 1) * 8 + (line >> 5)
    spread = dot(hot((lane == pick) & (line < 2 * OWNER_SLOTS)), tiles)
    spread = jnp.where((lane & 1) == (line & 1), spread, 0.0).astype(BF16)
    group = (COLUMNS * 8, LANES)
    labels = dot_nt(hot((iota(group, 1) >> 1) == (iota(group, 0) >> 3)), spread)
    labels = labels.reshape(COLUMNS, 8, LANES)
    out = jnp.concatenate([rows[:, :, :LANES], rows[:, :, LANES:], labels], axis=1).astype(BF16)
    for helper in range(HELPERS):
        send_ref[:, helper] = out


def best_kernel(got_ref, out_ref):
    helper = lax.axis_index("help")
    sources = COLUMNS * HELPERS
    total = sources * OWNER_SLOTS
    low = got_ref[:, :, :OWNER_SLOTS].reshape(total, LANES)
    high = got_ref[:, :, OWNER_SLOTS : 2 * OWNER_SLOTS].reshape(total, LANES)
    columns = jnp.concatenate([low, high], axis=1)
    own_low = got_ref[:, helper, :OWNER_SLOTS].reshape(SLAB, LANES)
    own_high = got_ref[:, helper, OWNER_SLOTS : 2 * OWNER_SLOTS].reshape(SLAB, LANES)

    dest = iota((SLAB, SLAB), 0)
    in_owner = ((dest >> 3) & 15) * SLOTS + (dest >> 7)
    order = hot(iota((SLAB, SLAB), 1) == ((dest & 7) ^ COLUMN_TURN) * OWNER_SLOTS + in_owner)
    own = dot(order, jnp.concatenate([own_low, own_high], axis=1)).astype(BF16)
    scores = dot_nt(own, columns)

    tiles = got_ref[...].astype(F32)[:, :, 2 * OWNER_SLOTS :].reshape(sources * 8, LANES).astype(BF16)
    shape = (total, sources * 8)
    spread = dot(hot(iota(shape, 1) == (iota(shape, 0) >> 5) * 8), tiles)
    line, lane = iota((total, LANES), 0) & 31, iota((total, LANES), 1)
    spread = jnp.where(lane == line, spread * 128.0, jnp.where(lane == line + 32, spread, 0.0))
    column_label = dot_nt(jnp.ones((8, LANES), BF16), spread.astype(BF16))[:1]

    shape = (SLAB, sources * 8)
    line = iota(shape, 0)
    own_spread = dot(hot(iota(shape, 1) == (((line & 7) ^ COLUMN_TURN) * HELPERS + helper) * 8), tiles)
    line, lane = iota((SLAB, LANES), 0), iota((SLAB, LANES), 1)
    line = ((line >> 3) & 15) * SLOTS + (line >> 7)
    own_label = jnp.sum(
        jnp.where(lane == line, own_spread * 128.0, jnp.where(lane == line + 32, own_spread, 0.0)),
        axis=1,
        keepdims=True,
    )
    own_label = jnp.where(own_label > 0.5, own_label, -1.0)
    line = iota((SLAB, 1), 0)
    own_index = (((line & 7) ^ COLUMN_TURN) * HELPERS + helper) * OWNER_SLOTS + ((line >> 3) & 15) * SLOTS + (line >> 7)
    allowed = (own_label == column_label) & (own_index != iota((SLAB, total), 1))
    best = jnp.max(jnp.where(allowed, scores, -1.0), axis=1, keepdims=True)
    half = SLAB // 2
    lane = iota(out_ref.shape, 1)
    out_ref[...] = jnp.where(lane == 0, best[:half], jnp.where(lane == 1, best[half:], 0.0))


def finish_kernel(got_ref, target_ref, live_ref, out_ref):
    got = got_ref[...]
    target = target_ref[:1]
    value = jnp.where((target & 1) == 0, got[:, 0:1], got[:, 1:2])
    value = jnp.where(iota(got.shape, 0) == (target >> 1), value, 0.0)
    value = jnp.sum(value, axis=0, keepdims=True)
    out_ref[...] = jnp.where(live_ref[...] == 1, value, -1.0)


VMEM = pl.BlockSpec(memory_space=pltpu.VMEM)
LIMIT = pltpu.CompilerParams(vmem_limit_bytes=32 * 1024 * 1024)


def shards(embeds, head_rows, cluster_of, owner_of, live_mask):
    row_count = embeds.shape[0]
    live = live_mask.reshape(1, row_count)
    packed = jnp.concatenate([owner_of, cluster_of, live_mask]).reshape(-1, LANES)
    target, hit, label = pl.pallas_call(
        index_kernel,
        out_shape=(
            jax.ShapeDtypeStruct((8, row_count), jnp.int32),
            jax.ShapeDtypeStruct((SLAB, row_count), BF16),
            jax.ShapeDtypeStruct((PLANES * 8, LANES), F32),
        ),
        in_specs=[VMEM],
        out_specs=(VMEM,) * 3,
        compiler_params=LIMIT,
        cost_estimate=pl.CostEstimate(flops=8_000_000_000, bytes_accessed=0, transcendentals=0),
        name="index",
    )(packed)
    embeds, hit = lax.optimization_barrier((embeds, hit))
    projected = jnp.dot(embeds, head_rows, preferred_element_type=F32)
    norm = lax.rsqrt(jnp.sum(projected * projected, axis=1, keepdims=True) + NORM_EPS)
    prefix = (projected * norm).astype(BF16)
    send = pl.pallas_call(
        scatter_kernel,
        out_shape=jax.ShapeDtypeStruct((PLANES, 2 * PIECES + 1, 4, LANES), BF16),
        in_specs=[VMEM] * 3,
        out_specs=VMEM,
        compiler_params=LIMIT,
        name="scatter",
    )(prefix, hit, label)
    planes = [[spot ^ PLANE_TURN for spot in range(PLANES)]]
    got = lax.all_to_all(
        send, "z", split_axis=0, concat_axis=0, tiled=True, axis_index_groups=planes
    )
    lines = 2 * OWNER_SLOTS + 8
    send = pl.pallas_call(
        sort_kernel,
        out_shape=jax.ShapeDtypeStruct((COLUMNS, HELPERS, lines, LANES), BF16),
        in_specs=[VMEM],
        out_specs=VMEM,
        compiler_params=LIMIT,
        name="sort",
    )(got)
    got = lax.all_to_all(
        send.reshape(COLUMNS * HELPERS, lines, LANES),
        ("x", "core", "help"),
        split_axis=0,
        concat_axis=0,
        tiled=True,
    )
    best = pl.pallas_call(
        best_kernel,
        out_shape=jax.ShapeDtypeStruct((PLANES * COLUMNS, LANES), F32),
        in_specs=[VMEM],
        out_specs=VMEM,
        compiler_params=LIMIT,
        name="best",
    )(got.reshape(COLUMNS, HELPERS, lines, LANES))
    turn = PLANE_TURN * COLUMNS + COLUMN_TURN
    owners = [[spot ^ turn for spot in range(PLANES * COLUMNS)]]
    back = lax.all_to_all(
        best, ("z", "x", "core"), split_axis=0, concat_axis=0, tiled=True, axis_index_groups=owners
    )
    nearest = pl.pallas_call(
        finish_kernel,
        out_shape=jax.ShapeDtypeStruct((1, row_count), F32),
        in_specs=[VMEM, VMEM, VMEM],
        out_specs=VMEM,
        compiler_params=LIMIT,
        name="finish",
    )(back, target, live)
    return (prefix, nearest.reshape(row_count))


def solution(mesh):
    axes = ("z", "x", "core", "help")
    fine = Mesh(mesh.devices.reshape(PLANES, 4, 2, HELPERS), axes)
    return jax.shard_map(
        shards,
        mesh=fine,
        in_specs=(P(axes, None), P(), P(axes), P(), P(axes)),
        out_specs=(P(axes, None), P(axes)),
        check_vma=False,
    )
```

```python
import jax
import jax.numpy as jnp
from jax import lax
from jax.experimental import pallas as pl
from jax.experimental.pallas import tpu as pltpu
from jax.sharding import Mesh, PartitionSpec as P

NORM_EPS = 1e-06
LANES = 128
PLANES = 16
COLUMNS = 8
HELPERS = 4
SLOTS = 2
PLANE_SLOTS = COLUMNS * SLOTS
SLAB = PLANES * PLANE_SLOTS
OWNER_SLOTS = PLANES * SLOTS
PIECES = 2 * PLANE_SLOTS // 8
PLANE_FIRST = 11
PLANE_TURN = 8
COLUMN_TURN = 4

F32 = jnp.float32
BF16 = jnp.bfloat16


def iota(shape, dim):
    return lax.broadcasted_iota(jnp.int32, shape, dim)


def hot(condition):
    return jnp.where(condition, 1.0, 0.0).astype(BF16)


def dot_nt(left, right):
    return lax.dot_general(left, right, (((1,), (1,)), ((), ())), preferred_element_type=F32)


def dot(left, right):
    return jnp.dot(left, right, preferred_element_type=F32)


def index_kernel(packed_ref, target_ref, hit_ref, label_ref):
    square = (LANES, LANES)
    cluster = packed_ref[16:17]
    high, low = cluster >> 7, cluster & 127
    by_low = dot(packed_ref[:16].astype(F32).astype(BF16), hot(iota(square, 0) == low))
    owner = jnp.sum(jnp.where(iota(by_low.shape, 0) == high, by_low, 0.0), axis=0, keepdims=True)
    owner = owner.astype(jnp.int32)
    owner_hot = hot(iota(square, 0) == owner)
    same = lax.dot_general(
        owner_hot, owner_hot, (((0,), (0,)), ((), ())), preferred_element_type=F32
    )
    slot = jnp.sum(jnp.where(iota(square, 0) < iota(square, 1), same, 0.0), axis=0, keepdims=True)
    target = owner * SLOTS + slot.astype(jnp.int32)
    back = target ^ (PLANE_TURN * PLANE_SLOTS + COLUMN_TURN * SLOTS)
    target_ref[...] = jnp.broadcast_to(back, target_ref.shape)
    target = (target - PLANE_FIRST * PLANE_SLOTS) & (SLAB - 1)

    live = packed_ref[17:18] == 1
    high_label = jnp.where(live, high + 1, 0)
    low_label = jnp.where(live, low, 0)
    line = iota(square, 0)
    part = jnp.where((line & 7) == 0, high_label, jnp.where((line & 7) == 1, low_label, 0))
    part = jnp.where((line >> 3) == (target >> 4), part, 0).astype(F32).astype(BF16)
    label_ref[...] = dot_nt(part, hot(line == (target & 15)))
    hit_ref[...] = hot(iota((SLAB, LANES), 0) == target)


def scatter_kernel(prefix_ref, hit_ref, label_ref, send_ref):
    rows = dot(hit_ref[...], prefix_ref[...]).reshape(PLANES, PLANE_SLOTS, 2 * LANES)
    rows = jnp.concatenate([rows[:, :, :LANES], rows[:, :, LANES:]], axis=1)
    rows = rows.reshape(PLANES, PIECES, 8, LANES)
    labels = label_ref[...].reshape(PLANES, 1, 8, LANES)
    send_ref[...] = jnp.concatenate(
        [rows[:, :, :4], rows[:, :, 4:], labels[:, :, :4]], axis=1
    ).astype(BF16)


def sort_kernel(got_ref, send_ref):
    pieces = got_ref[...].astype(F32)
    got = jnp.concatenate([pieces[:, :PIECES], pieces[:, PIECES : 2 * PIECES]], axis=2)
    got = got.reshape(PLANES, 2 * PLANE_SLOTS, LANES)
    low = got[:, :PLANE_SLOTS].reshape(SLAB, LANES).astype(BF16)
    high = got[:, PLANE_SLOTS:].reshape(SLAB, LANES).astype(BF16)
    dest = iota((SLAB, SLAB), 0)
    source = ((dest >> 1) & 15) * PLANE_SLOTS + (dest >> 5) * SLOTS + (dest & 1)
    order = hot(iota((SLAB, SLAB), 1) == source)
    rows = dot(order, jnp.concatenate([low, high], axis=1))
    rows = rows.reshape(COLUMNS, OWNER_SLOTS, 2 * LANES)

    square = (LANES, LANES)
    tiles = pieces[:, 2 * PIECES].reshape(PLANES, 4, LANES)
    tiles = jnp.concatenate([tiles, tiles], axis=1).reshape(PLANES * 8, LANES).astype(BF16)
    line, lane = iota(square, 0), iota(square, 1)
    pick = ((line & 31) >> 1) * 8 + (line >> 5)
    spread = dot(hot((lane == pick) & (line < 2 * OWNER_SLOTS)), tiles)
    spread = jnp.where((lane & 1) == (line & 1), spread, 0.0).astype(BF16)
    group = (COLUMNS * 8, LANES)
    labels = dot_nt(hot((iota(group, 1) >> 1) == (iota(group, 0) >> 3)), spread)
    labels = labels.reshape(COLUMNS, 8, LANES)
    out = jnp.concatenate([rows[:, :, :LANES], rows[:, :, LANES:], labels], axis=1).astype(BF16)
    for helper in range(HELPERS):
        send_ref[:, helper] = out


def from_first(plane_back):
    return (plane_back + PLANE_TURN - PLANE_FIRST) & (PLANES - 1)


def best_kernel(got_ref, out_ref):
    helper = lax.axis_index("help")
    sources = COLUMNS * HELPERS
    total = sources * OWNER_SLOTS
    low = got_ref[:, :, :OWNER_SLOTS].reshape(total, LANES)
    high = got_ref[:, :, OWNER_SLOTS : 2 * OWNER_SLOTS].reshape(total, LANES)
    columns = jnp.concatenate([low, high], axis=1)
    own_low = got_ref[:, helper, :OWNER_SLOTS].reshape(SLAB, LANES)
    own_high = got_ref[:, helper, OWNER_SLOTS : 2 * OWNER_SLOTS].reshape(SLAB, LANES)

    dest = iota((SLAB, SLAB), 0)
    in_owner = from_first(dest >> 3) * SLOTS + (dest >> 7)
    order = hot(iota((SLAB, SLAB), 1) == ((dest & 7) ^ COLUMN_TURN) * OWNER_SLOTS + in_owner)
    own = dot(order, jnp.concatenate([own_low, own_high], axis=1)).astype(BF16)
    scores = dot_nt(own, columns)

    tiles = got_ref[...].astype(F32)[:, :, 2 * OWNER_SLOTS :].reshape(sources * 8, LANES).astype(BF16)
    shape = (total, sources * 8)
    spread = dot(hot(iota(shape, 1) == (iota(shape, 0) >> 5) * 8), tiles)
    line, lane = iota((total, LANES), 0) & 31, iota((total, LANES), 1)
    spread = jnp.where(lane == line, spread * 128.0, jnp.where(lane == line + 32, spread, 0.0))
    column_label = dot_nt(jnp.ones((8, LANES), BF16), spread.astype(BF16))[:1]

    shape = (SLAB, sources * 8)
    line = iota(shape, 0)
    own_spread = dot(hot(iota(shape, 1) == (((line & 7) ^ COLUMN_TURN) * HELPERS + helper) * 8), tiles)
    line, lane = iota((SLAB, LANES), 0), iota((SLAB, LANES), 1)
    line = from_first(line >> 3) * SLOTS + (line >> 7)
    own_label = jnp.sum(
        jnp.where(lane == line, own_spread * 128.0, jnp.where(lane == line + 32, own_spread, 0.0)),
        axis=1,
        keepdims=True,
    )
    own_label = jnp.where(own_label > 0.5, own_label, -1.0)
    line = iota((SLAB, 1), 0)
    own_index = (((line & 7) ^ COLUMN_TURN) * HELPERS + helper) * OWNER_SLOTS + from_first(line >> 3) * SLOTS + (line >> 7)
    allowed = (own_label == column_label) & (own_index != iota((SLAB, total), 1))
    best = jnp.max(jnp.where(allowed, scores, -1.0), axis=1, keepdims=True)
    half = SLAB // 2
    lane = iota(out_ref.shape, 1)
    out_ref[...] = jnp.where(lane == 0, best[:half], jnp.where(lane == 1, best[half:], 0.0))


def finish_kernel(got_ref, target_ref, live_ref, out_ref):
    got = got_ref[...]
    target = target_ref[:1]
    value = jnp.where((target & 1) == 0, got[:, 0:1], got[:, 1:2])
    value = jnp.where(iota(got.shape, 0) == (target >> 1), value, 0.0)
    value = jnp.sum(value, axis=0, keepdims=True)
    out_ref[...] = jnp.where(live_ref[...] == 1, value, -1.0)


VMEM = pl.BlockSpec(memory_space=pltpu.VMEM)
LIMIT = pltpu.CompilerParams(vmem_limit_bytes=32 * 1024 * 1024)


def shards(embeds, head_rows, cluster_of, owner_of, live_mask):
    row_count = embeds.shape[0]
    live = live_mask.reshape(1, row_count)
    packed = jnp.concatenate([owner_of, cluster_of, live_mask]).reshape(-1, LANES)
    target, hit, label = pl.pallas_call(
        index_kernel,
        out_shape=(
            jax.ShapeDtypeStruct((8, row_count), jnp.int32),
            jax.ShapeDtypeStruct((SLAB, row_count), BF16),
            jax.ShapeDtypeStruct((PLANES * 8, LANES), F32),
        ),
        in_specs=[VMEM],
        out_specs=(VMEM,) * 3,
        compiler_params=LIMIT,
        cost_estimate=pl.CostEstimate(flops=8_000_000_000, bytes_accessed=0, transcendentals=0),
        name="index",
    )(packed)
    embeds, hit = lax.optimization_barrier((embeds, hit))
    projected = jnp.dot(embeds, head_rows, preferred_element_type=F32)
    norm = lax.rsqrt(jnp.sum(projected * projected, axis=1, keepdims=True) + NORM_EPS)
    prefix = (projected * norm).astype(BF16)
    send = pl.pallas_call(
        scatter_kernel,
        out_shape=jax.ShapeDtypeStruct((PLANES, 2 * PIECES + 1, 4, LANES), BF16),
        in_specs=[VMEM] * 3,
        out_specs=VMEM,
        compiler_params=LIMIT,
        name="scatter",
    )(prefix, hit, label)
    planes = [[(spot + PLANE_FIRST) % PLANES for spot in range(PLANES)]]
    got = lax.all_to_all(
        send, "z", split_axis=0, concat_axis=0, tiled=True, axis_index_groups=planes
    )
    lines = 2 * OWNER_SLOTS + 8
    send = pl.pallas_call(
        sort_kernel,
        out_shape=jax.ShapeDtypeStruct((COLUMNS, HELPERS, lines, LANES), BF16),
        in_specs=[VMEM],
        out_specs=VMEM,
        compiler_params=LIMIT,
        name="sort",
    )(got)
    got = lax.all_to_all(
        send.reshape(COLUMNS * HELPERS, lines, LANES),
        ("x", "core", "help"),
        split_axis=0,
        concat_axis=0,
        tiled=True,
    )
    best = pl.pallas_call(
        best_kernel,
        out_shape=jax.ShapeDtypeStruct((PLANES * COLUMNS, LANES), F32),
        in_specs=[VMEM],
        out_specs=VMEM,
        compiler_params=LIMIT,
        name="best",
    )(got.reshape(COLUMNS, HELPERS, lines, LANES))
    turn = PLANE_TURN * COLUMNS + COLUMN_TURN
    owners = [[spot ^ turn for spot in range(PLANES * COLUMNS)]]
    back = lax.all_to_all(
        best, ("z", "x", "core"), split_axis=0, concat_axis=0, tiled=True, axis_index_groups=owners
    )
    nearest = pl.pallas_call(
        finish_kernel,
        out_shape=jax.ShapeDtypeStruct((1, row_count), F32),
        in_specs=[VMEM, VMEM, VMEM],
        out_specs=VMEM,
        compiler_params=LIMIT,
        name="finish",
    )(back, target, live)
    return (prefix, nearest.reshape(row_count))


def solution(mesh):
    axes = ("z", "x", "core", "help")
    fine = Mesh(mesh.devices.reshape(PLANES, 4, 2, HELPERS), axes)
    return jax.shard_map(
        shards,
        mesh=fine,
        in_specs=(P(axes, None), P(), P(axes), P(), P(axes)),
        out_specs=(P(axes, None), P(axes)),
        check_vma=False,
    )
```

```python
import jax
import jax.numpy as jnp
from jax import lax
from jax.experimental import pallas as pl
from jax.experimental.pallas import tpu as pltpu
from jax.sharding import Mesh, PartitionSpec as P

NORM_EPS = 1e-06
LANES = 128
PLANES = 16
COLUMNS = 8
HELPERS = 4
SLOTS = 2
PLANE_SLOTS = COLUMNS * SLOTS
SLAB = PLANES * PLANE_SLOTS
OWNER_SLOTS = PLANES * SLOTS
PIECES = 2 * PLANE_SLOTS // 8
PLANE_TURN = 8
COLUMN_TURN = 4

F32 = jnp.float32
BF16 = jnp.bfloat16


def iota(shape, dim):
    return lax.broadcasted_iota(jnp.int32, shape, dim)


def hot(condition):
    return jnp.where(condition, 1.0, 0.0).astype(BF16)


def dot_nt(left, right):
    return lax.dot_general(left, right, (((1,), (1,)), ((), ())), preferred_element_type=F32)


def dot(left, right):
    return jnp.dot(left, right, preferred_element_type=F32)


def index_kernel(packed_ref, target_ref, hit_ref, label_ref):
    square = (LANES, LANES)
    cluster = packed_ref[16:17]
    high, low = cluster >> 7, cluster & 127
    by_low = dot(packed_ref[:16].astype(F32).astype(BF16), hot(iota(square, 0) == low))
    owner = jnp.sum(jnp.where(iota(by_low.shape, 0) == high, by_low, 0.0), axis=0, keepdims=True)
    owner = owner.astype(jnp.int32)
    owner_hot = hot(iota(square, 0) == owner)
    same = lax.dot_general(
        owner_hot, owner_hot, (((0,), (0,)), ((), ())), preferred_element_type=F32
    )
    slot = jnp.sum(jnp.where(iota(square, 0) < iota(square, 1), same, 0.0), axis=0, keepdims=True)
    target = owner * SLOTS + slot.astype(jnp.int32)
    target = target ^ (PLANE_TURN * PLANE_SLOTS)
    back = (((target >> 1) & 7) ^ COLUMN_TURN) * OWNER_SLOTS + (target >> 4) * SLOTS + (target & 1)
    target_ref[...] = jnp.broadcast_to(back, target_ref.shape)

    live = packed_ref[17:18] == 1
    high_label = jnp.where(live, high + 1, 0)
    low_label = jnp.where(live, low, 0)
    line = iota(square, 0)
    part = jnp.where((line & 7) == 0, high_label, jnp.where((line & 7) == 1, low_label, 0))
    part = jnp.where((line >> 3) == (target >> 4), part, 0).astype(F32).astype(BF16)
    label_ref[...] = dot_nt(part, hot(line == (target & 15)))
    hit_ref[...] = hot(iota((SLAB, LANES), 0) == target)


def scatter_kernel(prefix_ref, hit_ref, label_ref, send_ref):
    rows = dot(hit_ref[...], prefix_ref[...]).reshape(PLANES, PLANE_SLOTS, 2 * LANES)
    rows = jnp.concatenate([rows[:, :, :LANES], rows[:, :, LANES:]], axis=1)
    rows = rows.reshape(PLANES, PIECES, 8, LANES)
    labels = label_ref[...].reshape(PLANES, 1, 8, LANES)
    send_ref[...] = jnp.concatenate(
        [rows[:, :, :4], rows[:, :, 4:], labels[:, :, :4]], axis=1
    ).astype(BF16)


def sort_kernel(got_ref, send_ref):
    helper = lax.axis_index("help")
    pieces = got_ref[...].astype(F32)
    got = jnp.concatenate([pieces[:, :PIECES], pieces[:, PIECES : 2 * PIECES]], axis=2)
    got = got.reshape(PLANES, 2 * PLANE_SLOTS, LANES)
    low = got[:, :PLANE_SLOTS].reshape(SLAB, LANES).astype(BF16)
    high = got[:, PLANE_SLOTS:].reshape(SLAB, LANES).astype(BF16)
    dest = iota((SLAB, SLAB), 0)
    source = (dest & 15) * PLANE_SLOTS + (dest >> 5) * SLOTS + ((dest >> 4) & 1)
    order = hot(iota((SLAB, SLAB), 1) == source)
    rows = dot(order, jnp.concatenate([low, high], axis=1))
    rows = rows.reshape(COLUMNS, OWNER_SLOTS, 2 * LANES)

    tiles = pieces[:, 2 * PIECES].reshape(PLANES, 4, LANES)
    tiles = jnp.concatenate([tiles, tiles], axis=1).reshape(PLANES * 8, LANES).astype(BF16)
    line, lane = iota((2 * LANES, LANES), 0), iota((2 * LANES, LANES), 1)
    mine = ((line >> 5) & 3) == helper
    spread = dot(hot((lane == (line & 15) * 8 + (line >> 7)) & mine), tiles)
    spread = jnp.where((lane & 1) == ((line >> 4) & 1), spread, 0.0).astype(BF16)
    group = (COLUMNS * 8, LANES)
    labels = dot_nt(hot((iota(group, 1) >> 1) == (iota(group, 0) >> 3)), spread)
    labels = jnp.where((iota(group, 0) & 7) < 4, labels[:, :LANES], labels[:, LANES:])
    labels = labels.reshape(COLUMNS, 8, LANES)
    out = jnp.concatenate([rows[:, :, :LANES], rows[:, :, LANES:], labels], axis=1).astype(BF16)
    for helper in range(HELPERS):
        send_ref[:, helper] = out


def turned(blocks):
    return jnp.concatenate([blocks[COLUMN_TURN:], blocks[:COLUMN_TURN]], axis=0)


def best_kernel(got_ref, out_ref):
    helper = lax.axis_index("help")
    total = COLUMNS * HELPERS * OWNER_SLOTS
    low = got_ref[:, :, :OWNER_SLOTS].reshape(total, LANES)
    high = got_ref[:, :, OWNER_SLOTS : 2 * OWNER_SLOTS].reshape(total, LANES)

    own = got_ref[:, helper, : 2 * OWNER_SLOTS].reshape(COLUMNS, 2 * SLOTS, PLANES, LANES)
    own = turned(own)
    parts = [own[:, part].reshape(COLUMNS * PLANES, LANES) for part in range(2 * SLOTS)]
    own = jnp.concatenate(
        [jnp.concatenate(parts[:SLOTS], axis=0), jnp.concatenate(parts[SLOTS:], axis=0)], axis=1
    )
    scores = dot_nt(own, jnp.concatenate([low, high], axis=1))

    label = jnp.sum(got_ref[...].astype(F32)[:, :, 2 * OWNER_SLOTS :], axis=1)
    label = label[:, 0:1] * 128.0 + label[:, 4:5]
    shape = (SLOTS, COLUMNS, PLANES, LANES)
    small = (SLOTS, 1, PLANES, LANES)
    self_lane = iota(small, 3) == helper * OWNER_SLOTS + iota(small, 0) * PLANES + iota(small, 2)
    spread = jnp.where(self_lane, turned(label)[None], 0.0)
    own_label = jnp.sum(spread, axis=3, keepdims=True)
    own_label = jnp.where(own_label > 0.5, own_label, -1.0)
    best = jnp.full(shape, -1.0, F32)
    for column in range(COLUMNS):
        block = scores[:, column * LANES : (column + 1) * LANES].reshape(shape)
        block = jnp.where(own_label == label[column][None, None], block, -1.0)
        back = column ^ COLUMN_TURN
        no_self = jnp.where(self_lane, -1.0, block[:, back : back + 1])
        parts = [block[:, :back], no_self, block[:, back + 1 :]]
        best = jnp.maximum(best, jnp.concatenate([p for p in parts if p.shape[1]], axis=1))
    best = jnp.max(best, axis=3, keepdims=True).reshape(SLOTS, COLUMNS * PLANES, 1)
    lane = iota(out_ref.shape, 1)
    out_ref[...] = jnp.where(lane == 0, best[0], jnp.where(lane == 1, best[1], 0.0))


def finish_kernel(got_ref, target_ref, live_ref, out_ref):
    got = got_ref[...]
    target = target_ref[:1]
    value = jnp.where((target & 1) == 0, got[:, 0:1], got[:, 1:2])
    value = jnp.where(iota(got.shape, 0) == (target >> 1), value, 0.0)
    value = jnp.sum(value, axis=0, keepdims=True)
    out_ref[...] = jnp.where(live_ref[...] == 1, value, -1.0)


VMEM = pl.BlockSpec(memory_space=pltpu.VMEM)
LIMIT = pltpu.CompilerParams(vmem_limit_bytes=32 * 1024 * 1024)


def shards(embeds, head_rows, cluster_of, owner_of, live_mask):
    row_count = embeds.shape[0]
    live = live_mask.reshape(1, row_count)
    packed = jnp.concatenate([owner_of, cluster_of, live_mask]).reshape(-1, LANES)
    target, hit, label = pl.pallas_call(
        index_kernel,
        out_shape=(
            jax.ShapeDtypeStruct((8, row_count), jnp.int32),
            jax.ShapeDtypeStruct((SLAB, row_count), BF16),
            jax.ShapeDtypeStruct((PLANES * 8, LANES), F32),
        ),
        in_specs=[VMEM],
        out_specs=(VMEM,) * 3,
        compiler_params=LIMIT,
        cost_estimate=pl.CostEstimate(flops=700_000_000, bytes_accessed=0, transcendentals=0),
        name="index",
    )(packed)
    embeds, hit = lax.optimization_barrier((embeds, hit))
    projected = jnp.dot(embeds, head_rows, preferred_element_type=F32)
    norm = lax.rsqrt(jnp.sum(projected * projected, axis=1, keepdims=True) + NORM_EPS)
    prefix = (projected * norm).astype(BF16)
    send = pl.pallas_call(
        scatter_kernel,
        out_shape=jax.ShapeDtypeStruct((PLANES, 2 * PIECES + 1, 4, LANES), BF16),
        in_specs=[VMEM] * 3,
        out_specs=VMEM,
        compiler_params=LIMIT,
        name="scatter",
    )(prefix, hit, label)
    planes = [[spot ^ PLANE_TURN for spot in range(PLANES)]]
    got = lax.all_to_all(
        send, "z", split_axis=0, concat_axis=0, tiled=True, axis_index_groups=planes
    )
    lines = 2 * OWNER_SLOTS + 8
    send = pl.pallas_call(
        sort_kernel,
        out_shape=jax.ShapeDtypeStruct((COLUMNS, HELPERS, lines, LANES), BF16),
        in_specs=[VMEM],
        out_specs=VMEM,
        compiler_params=LIMIT,
        name="sort",
    )(got)
    got = lax.all_to_all(
        send.reshape(COLUMNS * HELPERS, lines, LANES),
        ("x", "core", "help"),
        split_axis=0,
        concat_axis=0,
        tiled=True,
    )
    best = pl.pallas_call(
        best_kernel,
        out_shape=jax.ShapeDtypeStruct((PLANES * COLUMNS, LANES), F32),
        in_specs=[VMEM],
        out_specs=VMEM,
        compiler_params=LIMIT,
        name="best",
    )(got.reshape(COLUMNS, HELPERS, lines, LANES))
    owners = [
        [
            (spot % PLANES ^ PLANE_TURN) * COLUMNS + (spot // PLANES ^ COLUMN_TURN)
            for spot in range(PLANES * COLUMNS)
        ]
    ]
    back = lax.all_to_all(
        best, ("z", "x", "core"), split_axis=0, concat_axis=0, tiled=True, axis_index_groups=owners
    )
    nearest = pl.pallas_call(
        finish_kernel,
        out_shape=jax.ShapeDtypeStruct((1, row_count), F32),
        in_specs=[VMEM, VMEM, VMEM],
        out_specs=VMEM,
        compiler_params=LIMIT,
        name="finish",
    )(back, target, live)
    return (prefix, nearest.reshape(row_count))


def solution(mesh):
    axes = ("z", "x", "core", "help")
    fine = Mesh(mesh.devices.reshape(PLANES, 4, 2, HELPERS), axes)
    return jax.shard_map(
        shards,
        mesh=fine,
        in_specs=(P(axes, None), P(), P(axes), P(), P(axes)),
        out_specs=(P(axes, None), P(axes)),
        check_vma=False,
    )
```

```python
import jax
import jax.numpy as jnp
from jax import lax
from jax.experimental import pallas as pl
from jax.experimental.pallas import tpu as pltpu
from jax.sharding import Mesh, PartitionSpec as P

NORM_EPS = 1e-06
LANES = 128
PLANES = 16
COLUMNS = 8
HELPERS = 4
SLOTS = 2
PLANE_SLOTS = COLUMNS * SLOTS
SLAB = PLANES * PLANE_SLOTS
OWNER_SLOTS = PLANES * SLOTS
PIECES = 2 * PLANE_SLOTS // 8
PLANE_TURN = 8
COLUMN_TURN = 5
HELPER_TURN = 2

F32 = jnp.float32
BF16 = jnp.bfloat16


def iota(shape, dim):
    return lax.broadcasted_iota(jnp.int32, shape, dim)


def hot(condition):
    return jnp.where(condition, 1.0, 0.0).astype(BF16)


def dot_nt(left, right):
    return lax.dot_general(left, right, (((1,), (1,)), ((), ())), preferred_element_type=F32)


def dot(left, right):
    return jnp.dot(left, right, preferred_element_type=F32)


def index_kernel(packed_ref, target_ref, hit_ref, label_ref):
    square = (LANES, LANES)
    cluster = packed_ref[16:17]
    high, low = cluster >> 7, cluster & 127
    by_low = dot(packed_ref[:16].astype(F32).astype(BF16), hot(iota(square, 0) == low))
    owner = jnp.sum(jnp.where(iota(by_low.shape, 0) == high, by_low, 0.0), axis=0, keepdims=True)
    owner = owner.astype(jnp.int32)
    owner_hot = hot(iota(square, 0) == owner)
    same = lax.dot_general(
        owner_hot, owner_hot, (((0,), (0,)), ((), ())), preferred_element_type=F32
    )
    slot = jnp.sum(jnp.where(iota(square, 0) < iota(square, 1), same, 0.0), axis=0, keepdims=True)
    target = owner * SLOTS + slot.astype(jnp.int32)
    target = target ^ (PLANE_TURN * PLANE_SLOTS)
    back = (((target >> 1) & 7) ^ COLUMN_TURN) * OWNER_SLOTS + (target >> 4) * SLOTS + (target & 1)
    target_ref[...] = jnp.broadcast_to(back, target_ref.shape)

    live = packed_ref[17:18] == 1
    high_label = jnp.where(live, high + 1, 0)
    low_label = jnp.where(live, low, 0)
    line = iota(square, 0)
    part = jnp.where((line & 7) == 0, high_label, jnp.where((line & 7) == 1, low_label, 0))
    part = jnp.where((line >> 3) == (target >> 4), part, 0).astype(F32).astype(BF16)
    label_ref[...] = dot_nt(part, hot(line == (target & 15)))
    hit_ref[...] = hot(iota((SLAB, LANES), 0) == target)


def scatter_kernel(prefix_ref, hit_ref, label_ref, send_ref):
    rows = dot(hit_ref[...], prefix_ref[...]).reshape(PLANES, PLANE_SLOTS, 2 * LANES)
    rows = jnp.concatenate([rows[:, :, :LANES], rows[:, :, LANES:]], axis=1)
    rows = rows.reshape(PLANES, PIECES, 8, LANES)
    labels = label_ref[...].reshape(PLANES, 1, 8, LANES)
    send_ref[...] = jnp.concatenate(
        [rows[:, :, :4], rows[:, :, 4:], labels[:, :, :4]], axis=1
    ).astype(BF16)


def sort_kernel(got_ref, send_ref):
    helper = lax.axis_index("help") ^ HELPER_TURN
    pieces = got_ref[...].astype(F32)
    got = jnp.concatenate([pieces[:, :PIECES], pieces[:, PIECES : 2 * PIECES]], axis=2)
    got = got.reshape(PLANES, 2 * PLANE_SLOTS, LANES)
    low = got[:, :PLANE_SLOTS].reshape(SLAB, LANES).astype(BF16)
    high = got[:, PLANE_SLOTS:].reshape(SLAB, LANES).astype(BF16)
    dest = iota((SLAB, SLAB), 0)
    source = (dest & 15) * PLANE_SLOTS + ((dest >> 5) ^ COLUMN_TURN) * SLOTS + ((dest >> 4) & 1)
    order = hot(iota((SLAB, SLAB), 1) == source)
    rows = dot(order, jnp.concatenate([low, high], axis=1))
    rows = rows.reshape(COLUMNS, OWNER_SLOTS, 2 * LANES)

    tiles = pieces[:, 2 * PIECES].reshape(PLANES, 4, LANES)
    tiles = jnp.concatenate([tiles, tiles], axis=1).reshape(PLANES * 8, LANES).astype(BF16)
    line, lane = iota((2 * LANES, LANES), 0), iota((2 * LANES, LANES), 1)
    mine = ((line >> 5) & 3) == helper
    spread = dot(hot((lane == (line & 15) * 8 + (line >> 7)) & mine), tiles)
    spread = jnp.where((lane & 1) == ((line >> 4) & 1), spread, 0.0).astype(BF16)
    group = (COLUMNS * 8, LANES)
    labels = dot_nt(hot((iota(group, 1) >> 1) == ((iota(group, 0) >> 3) ^ COLUMN_TURN)), spread)
    labels = jnp.where((iota(group, 0) & 7) < 4, labels[:, :LANES], labels[:, LANES:])
    labels = labels.reshape(COLUMNS, 8, LANES)
    out = jnp.concatenate([rows[:, :, :LANES], rows[:, :, LANES:], labels], axis=1).astype(BF16)
    for helper in range(HELPERS):
        send_ref[:, helper] = out


def best_kernel(got_ref, out_ref):
    helper = lax.axis_index("help") ^ HELPER_TURN
    total = COLUMNS * HELPERS * OWNER_SLOTS
    low = got_ref[:, :, :OWNER_SLOTS].reshape(total, LANES)
    high = got_ref[:, :, OWNER_SLOTS : 2 * OWNER_SLOTS].reshape(total, LANES)

    own = got_ref[:, helper, : 2 * OWNER_SLOTS].reshape(COLUMNS, 2 * SLOTS, PLANES, LANES)
    parts = [own[:, part].reshape(COLUMNS * PLANES, LANES) for part in range(2 * SLOTS)]
    own = jnp.concatenate(
        [jnp.concatenate(parts[:SLOTS], axis=0), jnp.concatenate(parts[SLOTS:], axis=0)], axis=1
    )
    scores = dot_nt(own, jnp.concatenate([low, high], axis=1))

    label = jnp.sum(got_ref[...].astype(F32)[:, :, 2 * OWNER_SLOTS :], axis=1)
    label = label[:, 0:1] * 128.0 + label[:, 4:5]
    shape = (SLOTS, COLUMNS, PLANES, LANES)
    small = (SLOTS, 1, PLANES, LANES)
    self_lane = iota(small, 3) == helper * OWNER_SLOTS + iota(small, 0) * PLANES + iota(small, 2)
    spread = jnp.where(self_lane, label[None], 0.0)
    own_label = jnp.sum(spread, axis=3, keepdims=True)
    own_label = jnp.where(own_label > 0.5, own_label, -1.0)
    best = jnp.full(shape, -1.0, F32)
    for column in range(COLUMNS):
        block = scores[:, column * LANES : (column + 1) * LANES].reshape(shape)
        block = jnp.where(own_label == label[column][None, None], block, -1.0)
        no_self = jnp.where(self_lane, -1.0, block[:, column : column + 1])
        parts = [block[:, :column], no_self, block[:, column + 1 :]]
        best = jnp.maximum(best, jnp.concatenate([p for p in parts if p.shape[1]], axis=1))
    best = jnp.max(best, axis=3, keepdims=True).reshape(SLOTS, COLUMNS * PLANES, 1)
    lane = iota(out_ref.shape, 1)
    out_ref[...] = jnp.where(lane == 0, best[0], jnp.where(lane == 1, best[1], 0.0))


def finish_kernel(got_ref, target_ref, live_ref, out_ref):
    got = got_ref[...]
    target = target_ref[:1]
    value = jnp.where((target & 1) == 0, got[:, 0:1], got[:, 1:2])
    value = jnp.where(iota(got.shape, 0) == (target >> 1), value, 0.0)
    value = jnp.sum(value, axis=0, keepdims=True)
    out_ref[...] = jnp.where(live_ref[...] == 1, value, -1.0)


VMEM = pl.BlockSpec(memory_space=pltpu.VMEM)
LIMIT = pltpu.CompilerParams(vmem_limit_bytes=32 * 1024 * 1024)


def shards(embeds, head_rows, cluster_of, owner_of, live_mask):
    row_count = embeds.shape[0]
    live = live_mask.reshape(1, row_count)
    packed = jnp.concatenate([owner_of, cluster_of, live_mask]).reshape(-1, LANES)
    target, hit, label = pl.pallas_call(
        index_kernel,
        out_shape=(
            jax.ShapeDtypeStruct((8, row_count), jnp.int32),
            jax.ShapeDtypeStruct((SLAB, row_count), BF16),
            jax.ShapeDtypeStruct((PLANES * 8, LANES), F32),
        ),
        in_specs=[VMEM],
        out_specs=(VMEM,) * 3,
        compiler_params=LIMIT,
        cost_estimate=pl.CostEstimate(flops=700_000_000, bytes_accessed=0, transcendentals=0),
        name="index",
    )(packed)
    embeds, hit = lax.optimization_barrier((embeds, hit))
    projected = jnp.dot(embeds, head_rows, preferred_element_type=F32)
    norm = lax.rsqrt(jnp.sum(projected * projected, axis=1, keepdims=True) + NORM_EPS)
    prefix = (projected * norm).astype(BF16)
    send = pl.pallas_call(
        scatter_kernel,
        out_shape=jax.ShapeDtypeStruct((PLANES, 2 * PIECES + 1, 4, LANES), BF16),
        in_specs=[VMEM] * 3,
        out_specs=VMEM,
        compiler_params=LIMIT,
        name="scatter",
    )(prefix, hit, label)
    planes = [[spot ^ PLANE_TURN for spot in range(PLANES)]]
    got = lax.all_to_all(
        send, "z", split_axis=0, concat_axis=0, tiled=True, axis_index_groups=planes
    )
    lines = 2 * OWNER_SLOTS + 8
    send = pl.pallas_call(
        sort_kernel,
        out_shape=jax.ShapeDtypeStruct((COLUMNS, HELPERS, lines, LANES), BF16),
        in_specs=[VMEM],
        out_specs=VMEM,
        compiler_params=LIMIT,
        name="sort",
    )(got)
    turn = COLUMN_TURN * HELPERS + HELPER_TURN
    members = [[spot ^ turn for spot in range(COLUMNS * HELPERS)]]
    got = lax.all_to_all(
        send.reshape(COLUMNS * HELPERS, lines, LANES),
        ("x", "core", "help"),
        split_axis=0,
        concat_axis=0,
        tiled=True,
        axis_index_groups=members,
    )
    best = pl.pallas_call(
        best_kernel,
        out_shape=jax.ShapeDtypeStruct((PLANES * COLUMNS, LANES), F32),
        in_specs=[VMEM],
        out_specs=VMEM,
        compiler_params=LIMIT,
        name="best",
    )(got.reshape(COLUMNS, HELPERS, lines, LANES))
    owners = [
        [
            (spot % PLANES ^ PLANE_TURN) * COLUMNS + (spot // PLANES ^ COLUMN_TURN)
            for spot in range(PLANES * COLUMNS)
        ]
    ]
    back = lax.all_to_all(
        best, ("z", "x", "core"), split_axis=0, concat_axis=0, tiled=True, axis_index_groups=owners
    )
    nearest = pl.pallas_call(
        finish_kernel,
        out_shape=jax.ShapeDtypeStruct((1, row_count), F32),
        in_specs=[VMEM, VMEM, VMEM],
        out_specs=VMEM,
        compiler_params=LIMIT,
        name="finish",
    )(back, target, live)
    return (prefix, nearest.reshape(row_count))


def solution(mesh):
    axes = ("z", "x", "core", "help")
    fine = Mesh(mesh.devices.reshape(PLANES, 4, 2, HELPERS), axes)
    return jax.shard_map(
        shards,
        mesh=fine,
        in_specs=(P(axes, None), P(), P(axes), P(), P(axes)),
        out_specs=(P(axes, None), P(axes)),
        check_vma=False,
    )
```

```python
import jax
import jax.numpy as jnp
from jax import lax
from jax.experimental import pallas as pl
from jax.experimental.pallas import tpu as pltpu
from jax.sharding import Mesh, PartitionSpec as P

NORM_EPS = 1e-06
LANES = 128
PLANES = 16
COLUMNS = 8
HELPERS = 4
SLOTS = 2
PLANE_SLOTS = COLUMNS * SLOTS
SLAB = PLANES * PLANE_SLOTS
OWNER_SLOTS = PLANES * SLOTS
PIECES = 2 * PLANE_SLOTS // 8
PLANE_TURN = 8
COLUMN_TURN = 5
HELPER_TURN = 2

F32 = jnp.float32
BF16 = jnp.bfloat16


def iota(shape, dim):
    return lax.broadcasted_iota(jnp.int32, shape, dim)


def column_at(place):
    return ((place & 3) * 2 + (place >> 2)) ^ COLUMN_TURN


def place_of(column):
    turned = column ^ COLUMN_TURN
    return (turned & 1) * 4 + (turned >> 1)


def hot(condition):
    return jnp.where(condition, 1.0, 0.0).astype(BF16)


def dot_nt(left, right):
    return lax.dot_general(left, right, (((1,), (1,)), ((), ())), preferred_element_type=F32)


def dot(left, right):
    return jnp.dot(left, right, preferred_element_type=F32)


def index_kernel(packed_ref, target_ref, hit_ref, label_ref):
    square = (LANES, LANES)
    cluster = packed_ref[16:17]
    high, low = cluster >> 7, cluster & 127
    by_low = dot(packed_ref[:16].astype(F32).astype(BF16), hot(iota(square, 0) == low))
    owner = jnp.sum(jnp.where(iota(by_low.shape, 0) == high, by_low, 0.0), axis=0, keepdims=True)
    owner = owner.astype(jnp.int32)
    owner_hot = hot(iota(square, 0) == owner)
    same = lax.dot_general(
        owner_hot, owner_hot, (((0,), (0,)), ((), ())), preferred_element_type=F32
    )
    slot = jnp.sum(jnp.where(iota(square, 0) < iota(square, 1), same, 0.0), axis=0, keepdims=True)
    target = owner * SLOTS + slot.astype(jnp.int32)
    target = target ^ (PLANE_TURN * PLANE_SLOTS)
    back = place_of((target >> 1) & 7) * OWNER_SLOTS + (target >> 4) * SLOTS + (target & 1)
    target_ref[...] = jnp.broadcast_to(back, target_ref.shape)

    live = packed_ref[17:18] == 1
    high_label = jnp.where(live, high + 1, 0)
    low_label = jnp.where(live, low, 0)
    line = iota(square, 0)
    part = jnp.where((line & 7) == 0, high_label, jnp.where((line & 7) == 1, low_label, 0))
    part = jnp.where((line >> 3) == (target >> 4), part, 0).astype(F32).astype(BF16)
    label_ref[...] = dot_nt(part, hot(line == (target & 15)))
    hit_ref[...] = hot(iota((SLAB, LANES), 0) == target)


def scatter_kernel(prefix_ref, hit_ref, label_ref, send_ref):
    rows = dot(hit_ref[...], prefix_ref[...]).reshape(PLANES, PLANE_SLOTS, 2 * LANES)
    rows = jnp.concatenate([rows[:, :, :LANES], rows[:, :, LANES:]], axis=1)
    rows = rows.reshape(PLANES, PIECES, 8, LANES)
    labels = label_ref[...].reshape(PLANES, 1, 8, LANES)
    parts = [rows[:, :, line : line + 2] for line in range(0, 8, 2)] + [labels[:, :, :2]]
    send_ref[...] = jnp.concatenate(parts, axis=1).astype(BF16)


def sort_kernel(got_ref, send_ref):
    helper = lax.axis_index("help") ^ HELPER_TURN
    pieces = got_ref[...].astype(F32)
    got = [pieces[:, part * PIECES : (part + 1) * PIECES] for part in range(4)]
    got = jnp.concatenate(got, axis=2)
    got = got.reshape(PLANES, 2 * PLANE_SLOTS, LANES)
    low = got[:, :PLANE_SLOTS].reshape(SLAB, LANES).astype(BF16)
    high = got[:, PLANE_SLOTS:].reshape(SLAB, LANES).astype(BF16)
    dest = iota((SLAB, SLAB), 0)
    source = (dest & 15) * PLANE_SLOTS + column_at(dest >> 5) * SLOTS + ((dest >> 4) & 1)
    order = hot(iota((SLAB, SLAB), 1) == source)
    rows = dot(order, jnp.concatenate([low, high], axis=1))
    rows = rows.reshape(COLUMNS, OWNER_SLOTS, 2 * LANES)

    tiles = jnp.concatenate([pieces[:, 4 * PIECES]] * 4, axis=1)
    tiles = tiles.reshape(PLANES * 8, LANES).astype(BF16)
    line, lane = iota((2 * LANES, LANES), 0), iota((2 * LANES, LANES), 1)
    mine = ((line >> 5) & 3) == helper
    spread = dot(hot((lane == (line & 15) * 8 + (line >> 7)) & mine), tiles)
    spread = jnp.where((lane & 1) == ((line >> 4) & 1), spread, 0.0).astype(BF16)
    group = (COLUMNS * 8, LANES)
    labels = dot_nt(hot((iota(group, 1) >> 1) == column_at(iota(group, 0) >> 3)), spread)
    labels = jnp.where((iota(group, 0) & 7) < 4, labels[:, :LANES], labels[:, LANES:])
    labels = labels.reshape(COLUMNS, 8, LANES)
    out = jnp.concatenate([rows[:, :, :LANES], rows[:, :, LANES:], labels], axis=1).astype(BF16)
    for helper in range(HELPERS):
        send_ref[:, helper] = out


def best_kernel(got_ref, out_ref):
    helper = lax.axis_index("help") ^ HELPER_TURN
    total = COLUMNS * HELPERS * OWNER_SLOTS
    low = got_ref[:, :, :OWNER_SLOTS].reshape(total, LANES)
    high = got_ref[:, :, OWNER_SLOTS : 2 * OWNER_SLOTS].reshape(total, LANES)

    own = got_ref[:, helper, : 2 * OWNER_SLOTS].reshape(COLUMNS, 2 * SLOTS, PLANES, LANES)
    parts = [own[:, part].reshape(COLUMNS * PLANES, LANES) for part in range(2 * SLOTS)]
    own = jnp.concatenate(
        [jnp.concatenate(parts[:SLOTS], axis=0), jnp.concatenate(parts[SLOTS:], axis=0)], axis=1
    )
    scores = dot_nt(own, jnp.concatenate([low, high], axis=1))

    label = jnp.sum(got_ref[...].astype(F32)[:, :, 2 * OWNER_SLOTS :], axis=1)
    label = label[:, 0:1] * 128.0 + label[:, 4:5]
    shape = (SLOTS, COLUMNS, PLANES, LANES)
    small = (SLOTS, 1, PLANES, LANES)
    self_lane = iota(small, 3) == helper * OWNER_SLOTS + iota(small, 0) * PLANES + iota(small, 2)
    spread = jnp.where(self_lane, label[None], 0.0)
    own_label = jnp.sum(spread, axis=3, keepdims=True)
    own_label = jnp.where(own_label > 0.5, own_label, -1.0)
    best = jnp.full(shape, -1.0, F32)
    for column in range(COLUMNS):
        block = scores[:, column * LANES : (column + 1) * LANES].reshape(shape)
        block = jnp.where(own_label == label[column][None, None], block, -1.0)
        no_self = jnp.where(self_lane, -1.0, block[:, column : column + 1])
        parts = [block[:, :column], no_self, block[:, column + 1 :]]
        best = jnp.maximum(best, jnp.concatenate([p for p in parts if p.shape[1]], axis=1))
    best = jnp.max(best, axis=3, keepdims=True).reshape(SLOTS, COLUMNS * PLANES, 1)
    lane = iota(out_ref.shape, 1)
    out_ref[...] = jnp.where(lane == 0, best[0], jnp.where(lane == 1, best[1], 0.0))


def finish_kernel(got_ref, target_ref, live_ref, out_ref):
    got = got_ref[...]
    target = target_ref[:1]
    value = jnp.where((target & 1) == 0, got[:, 0:1], got[:, 1:2])
    value = jnp.where(iota(got.shape, 0) == (target >> 1), value, 0.0)
    value = jnp.sum(value, axis=0, keepdims=True)
    out_ref[...] = jnp.where(live_ref[...] == 1, value, -1.0)


VMEM = pl.BlockSpec(memory_space=pltpu.VMEM)
LIMIT = pltpu.CompilerParams(vmem_limit_bytes=32 * 1024 * 1024)


def shards(embeds, head_rows, cluster_of, owner_of, live_mask):
    row_count = embeds.shape[0]
    live = live_mask.reshape(1, row_count)
    packed = jnp.concatenate([owner_of, cluster_of, live_mask]).reshape(-1, LANES)
    target, hit, label = pl.pallas_call(
        index_kernel,
        out_shape=(
            jax.ShapeDtypeStruct((8, row_count), jnp.int32),
            jax.ShapeDtypeStruct((SLAB, row_count), BF16),
            jax.ShapeDtypeStruct((PLANES * 8, LANES), F32),
        ),
        in_specs=[VMEM],
        out_specs=(VMEM,) * 3,
        compiler_params=LIMIT,
        cost_estimate=pl.CostEstimate(flops=700_000_000, bytes_accessed=0, transcendentals=0),
        name="index",
    )(packed)
    embeds, hit = lax.optimization_barrier((embeds, hit))
    projected = jnp.dot(embeds, head_rows, preferred_element_type=F32)
    norm = lax.rsqrt(jnp.sum(projected * projected, axis=1, keepdims=True) + NORM_EPS)
    prefix = (projected * norm).astype(BF16)
    send = pl.pallas_call(
        scatter_kernel,
        out_shape=jax.ShapeDtypeStruct((PLANES, 4 * PIECES + 1, 2, LANES), BF16),
        in_specs=[VMEM] * 3,
        out_specs=VMEM,
        compiler_params=LIMIT,
        name="scatter",
    )(prefix, hit, label)
    planes = [[spot ^ PLANE_TURN for spot in range(PLANES)]]
    got = lax.all_to_all(
        send, "z", split_axis=0, concat_axis=0, tiled=True, axis_index_groups=planes
    )
    lines = 2 * OWNER_SLOTS + 8
    send = pl.pallas_call(
        sort_kernel,
        out_shape=jax.ShapeDtypeStruct((COLUMNS, HELPERS, lines, LANES), BF16),
        in_specs=[VMEM],
        out_specs=VMEM,
        compiler_params=LIMIT,
        name="sort",
    )(got)
    members = [
        [
            column_at(spot // HELPERS) * HELPERS + (spot % HELPERS ^ HELPER_TURN)
            for spot in range(COLUMNS * HELPERS)
        ]
    ]
    got = lax.all_to_all(
        send.reshape(COLUMNS * HELPERS, lines, LANES),
        ("x", "core", "help"),
        split_axis=0,
        concat_axis=0,
        tiled=True,
        axis_index_groups=members,
    )
    best = pl.pallas_call(
        best_kernel,
        out_shape=jax.ShapeDtypeStruct((PLANES * COLUMNS, LANES), F32),
        in_specs=[VMEM],
        out_specs=VMEM,
        compiler_params=LIMIT,
        name="best",
    )(got.reshape(COLUMNS, HELPERS, lines, LANES))
    owners = [
        [
            (spot % PLANES ^ PLANE_TURN) * COLUMNS + column_at(spot // PLANES)
            for spot in range(PLANES * COLUMNS)
        ]
    ]
    back = lax.all_to_all(
        best, ("z", "x", "core"), split_axis=0, concat_axis=0, tiled=True, axis_index_groups=owners
    )
    nearest = pl.pallas_call(
        finish_kernel,
        out_shape=jax.ShapeDtypeStruct((1, row_count), F32),
        in_specs=[VMEM, VMEM, VMEM],
        out_specs=VMEM,
        compiler_params=LIMIT,
        name="finish",
    )(back, target, live)
    return (prefix, nearest.reshape(row_count))


def solution(mesh):
    axes = ("z", "x", "core", "help")
    fine = Mesh(mesh.devices.reshape(PLANES, 4, 2, HELPERS), axes)
    return jax.shard_map(
        shards,
        mesh=fine,
        in_specs=(P(axes, None), P(), P(axes), P(), P(axes)),
        out_specs=(P(axes, None), P(axes)),
        check_vma=False,
    )
```

```python
import jax
import jax.numpy as jnp
from jax import lax
from jax.experimental import pallas as pl
from jax.experimental.pallas import tpu as pltpu
from jax.sharding import Mesh, PartitionSpec as P

NORM_EPS = 1e-06
LANES = 128
PLANES = 16
COLUMNS = 8
HELPERS = 4
SLOTS = 2
PLANE_SLOTS = COLUMNS * SLOTS
SLAB = PLANES * PLANE_SLOTS
OWNER_SLOTS = PLANES * SLOTS
CHUNK = 2 * OWNER_SLOTS + 2
PIECES = 2 * PLANE_SLOTS // 8
PLANE_TURN = 8
COLUMN_TURN = 5
HELPER_TURN = 2

F32 = jnp.float32
BF16 = jnp.bfloat16


def iota(shape, dim):
    return lax.broadcasted_iota(jnp.int32, shape, dim)


def column_at(place):
    return ((place & 3) * 2 + (place >> 2)) ^ COLUMN_TURN


def place_of(column):
    turned = column ^ COLUMN_TURN
    return (turned & 1) * 4 + (turned >> 1)


def hot(condition):
    return jnp.where(condition, 1.0, 0.0).astype(BF16)


def dot_nt(left, right):
    return lax.dot_general(left, right, (((1,), (1,)), ((), ())), preferred_element_type=F32)


def dot(left, right):
    return jnp.dot(left, right, preferred_element_type=F32)


def index_kernel(packed_ref, target_ref, hit_ref, label_ref):
    square = (LANES, LANES)
    cluster = packed_ref[16:17]
    high, low = cluster >> 7, cluster & 127
    by_low = dot(packed_ref[:16].astype(F32).astype(BF16), hot(iota(square, 0) == low))
    owner = jnp.sum(jnp.where(iota(by_low.shape, 0) == high, by_low, 0.0), axis=0, keepdims=True)
    owner = owner.astype(jnp.int32)
    owner_hot = hot(iota(square, 0) == owner)
    same = lax.dot_general(
        owner_hot, owner_hot, (((0,), (0,)), ((), ())), preferred_element_type=F32
    )
    slot = jnp.sum(jnp.where(iota(square, 0) < iota(square, 1), same, 0.0), axis=0, keepdims=True)
    target = owner * SLOTS + slot.astype(jnp.int32)
    target = target ^ (PLANE_TURN * PLANE_SLOTS)
    back = place_of((target >> 1) & 7) * OWNER_SLOTS + (target >> 4) * SLOTS + (target & 1)
    target_ref[...] = jnp.broadcast_to(back, target_ref.shape)

    live = packed_ref[17:18] == 1
    high_label = jnp.where(live, high + 1, 0)
    low_label = jnp.where(live, low, 0)
    line = iota(square, 0)
    part = jnp.where((line & 7) == 0, high_label, jnp.where((line & 7) == 1, low_label, 0))
    part = jnp.where((line >> 3) == (target >> 4), part, 0).astype(F32).astype(BF16)
    label_ref[...] = dot_nt(part, hot(line == (target & 15)))
    hit_ref[...] = hot(iota((SLAB, LANES), 0) == target)


def scatter_kernel(prefix_ref, hit_ref, label_ref, send_ref):
    rows = dot(hit_ref[...], prefix_ref[...]).reshape(PLANES, PLANE_SLOTS, 2 * LANES)
    rows = jnp.concatenate([rows[:, :, :LANES], rows[:, :, LANES:]], axis=1)
    rows = rows.reshape(PLANES, PIECES, 8, LANES)
    labels = label_ref[...].reshape(PLANES, 1, 8, LANES)
    parts = [rows[:, :, line : line + 2] for line in range(0, 8, 2)] + [labels[:, :, :2]]
    send_ref[...] = jnp.concatenate(parts, axis=1).astype(BF16)


def sort_kernel(got_ref, send_ref):
    helper = lax.axis_index("help") ^ HELPER_TURN
    pieces = got_ref[...].astype(F32)
    got = [pieces[:, part * PIECES : (part + 1) * PIECES] for part in range(4)]
    got = jnp.concatenate(got, axis=2)
    got = got.reshape(PLANES, 2 * PLANE_SLOTS, LANES)
    low = got[:, :PLANE_SLOTS].reshape(SLAB, LANES).astype(BF16)
    high = got[:, PLANE_SLOTS:].reshape(SLAB, LANES).astype(BF16)
    dest = iota((SLAB, SLAB), 0)
    source = (dest & 15) * PLANE_SLOTS + column_at(dest >> 5) * SLOTS + ((dest >> 4) & 1)
    order = hot(iota((SLAB, SLAB), 1) == source)
    rows = dot(order, jnp.concatenate([low, high], axis=1))
    rows = rows.reshape(COLUMNS, OWNER_SLOTS, 2 * LANES)

    tiles = jnp.concatenate([pieces[:, 4 * PIECES]] * 4, axis=1)
    tiles = tiles.reshape(PLANES * 8, LANES).astype(BF16)
    line, lane = iota((2 * LANES, LANES), 0), iota((2 * LANES, LANES), 1)
    mine = ((line >> 5) & 3) == helper
    spread = dot(hot((lane == (line & 15) * 8 + (line >> 7)) & mine), tiles)
    spread = jnp.where((lane & 1) == ((line >> 4) & 1), spread, 0.0).astype(BF16)
    group = (COLUMNS * 8, LANES)
    labels = dot_nt(hot((iota(group, 1) >> 1) == column_at(iota(group, 0) >> 3)), spread)
    labels = jnp.where((iota(group, 0) & 7) == 0, labels[:, :LANES], labels[:, LANES:])
    labels = labels.reshape(COLUMNS, 8, LANES)
    parts = []
    for column in range(COLUMNS):
        chunk = [rows[column, :, :LANES], rows[column, :, LANES:], labels[column, :2]]
        parts += [part.astype(BF16) for part in chunk] * HELPERS
    send_ref[...] = jnp.concatenate(parts, axis=0)


def best_kernel(got_ref, out_ref):
    helper = lax.axis_index("help") ^ HELPER_TURN
    got = got_ref[...]
    lows, highs, owns, labels = [], [], [], []
    for column in range(COLUMNS):
        own = label = None
        for place in range(HELPERS):
            start = (column * HELPERS + place) * CHUNK
            chunk = got[start : start + 2 * OWNER_SLOTS]
            lows.append(chunk[:OWNER_SLOTS])
            highs.append(chunk[OWNER_SLOTS:])
            own = chunk if own is None else jnp.where(helper == place, chunk, own)
            part = got[start + 2 * OWNER_SLOTS : start + CHUNK].astype(F32)
            label = part if label is None else label + part
        owns.append(own)
        labels.append(label[0:1] * 128.0 + label[1:2])
    columns = jnp.concatenate(
        [jnp.concatenate(lows, axis=0), jnp.concatenate(highs, axis=0)], axis=1
    )

    parts = [
        jnp.concatenate([own[part * PLANES : (part + 1) * PLANES] for own in owns], axis=0)
        for part in range(2 * SLOTS)
    ]
    own = jnp.concatenate(
        [jnp.concatenate(parts[:SLOTS], axis=0), jnp.concatenate(parts[SLOTS:], axis=0)], axis=1
    )
    scores = dot_nt(own, columns)

    label = jnp.concatenate(labels, axis=0).reshape(COLUMNS, 1, LANES)
    shape = (SLOTS, COLUMNS, PLANES, LANES)
    small = (SLOTS, 1, PLANES, LANES)
    self_lane = iota(small, 3) == helper * OWNER_SLOTS + iota(small, 0) * PLANES + iota(small, 2)
    spread = jnp.where(self_lane, label[None], 0.0)
    own_label = jnp.sum(spread, axis=3, keepdims=True)
    own_label = jnp.where(own_label > 0.5, own_label, -1.0)
    best = jnp.full(shape, -1.0, F32)
    for column in range(COLUMNS):
        block = scores[:, column * LANES : (column + 1) * LANES].reshape(shape)
        block = jnp.where(own_label == label[column][None, None], block, -1.0)
        no_self = jnp.where(self_lane, -1.0, block[:, column : column + 1])
        parts = [block[:, :column], no_self, block[:, column + 1 :]]
        best = jnp.maximum(best, jnp.concatenate([p for p in parts if p.shape[1]], axis=1))
    best = jnp.max(best, axis=3, keepdims=True).reshape(SLOTS, COLUMNS * PLANES, 1)
    lane = iota(out_ref.shape, 1)
    out_ref[...] = jnp.where(lane == 0, best[0], jnp.where(lane == 1, best[1], 0.0))


def finish_kernel(got_ref, target_ref, live_ref, out_ref):
    got = got_ref[...]
    target = target_ref[:1]
    value = jnp.where((target & 1) == 0, got[:, 0:1], got[:, 1:2])
    value = jnp.where(iota(got.shape, 0) == (target >> 1), value, 0.0)
    value = jnp.sum(value, axis=0, keepdims=True)
    out_ref[...] = jnp.where(live_ref[...] == 1, value, -1.0)


VMEM = pl.BlockSpec(memory_space=pltpu.VMEM)
LIMIT = pltpu.CompilerParams(vmem_limit_bytes=32 * 1024 * 1024)


def shards(embeds, head_rows, cluster_of, owner_of, live_mask):
    row_count = embeds.shape[0]
    live = live_mask.reshape(1, row_count)
    packed = jnp.concatenate([owner_of, cluster_of, live_mask]).reshape(-1, LANES)
    target, hit, label = pl.pallas_call(
        index_kernel,
        out_shape=(
            jax.ShapeDtypeStruct((8, row_count), jnp.int32),
            jax.ShapeDtypeStruct((SLAB, row_count), BF16),
            jax.ShapeDtypeStruct((PLANES * 8, LANES), F32),
        ),
        in_specs=[VMEM],
        out_specs=(VMEM,) * 3,
        compiler_params=LIMIT,
        cost_estimate=pl.CostEstimate(flops=700_000_000, bytes_accessed=0, transcendentals=0),
        name="index",
    )(packed)
    embeds, hit = lax.optimization_barrier((embeds, hit))
    projected = jnp.dot(embeds, head_rows, preferred_element_type=F32)
    norm = lax.rsqrt(jnp.sum(projected * projected, axis=1, keepdims=True) + NORM_EPS)
    prefix = (projected * norm).astype(BF16)
    send = pl.pallas_call(
        scatter_kernel,
        out_shape=jax.ShapeDtypeStruct((PLANES, 4 * PIECES + 1, 2, LANES), BF16),
        in_specs=[VMEM] * 3,
        out_specs=VMEM,
        compiler_params=LIMIT,
        name="scatter",
    )(prefix, hit, label)
    planes = [[spot ^ PLANE_TURN for spot in range(PLANES)]]
    got = lax.all_to_all(
        send, "z", split_axis=0, concat_axis=0, tiled=True, axis_index_groups=planes
    )
    lines = COLUMNS * HELPERS * CHUNK
    send = pl.pallas_call(
        sort_kernel,
        out_shape=jax.ShapeDtypeStruct((lines, LANES), BF16),
        in_specs=[VMEM],
        out_specs=VMEM,
        compiler_params=LIMIT,
        name="sort",
    )(got)
    members = [
        [
            column_at(spot // HELPERS) * HELPERS + (spot % HELPERS ^ HELPER_TURN)
            for spot in range(COLUMNS * HELPERS)
        ]
    ]
    got = lax.all_to_all(
        send.reshape(COLUMNS * HELPERS, CHUNK // 2, 2, LANES),
        ("x", "core", "help"),
        split_axis=0,
        concat_axis=0,
        tiled=True,
        axis_index_groups=members,
    )
    best = pl.pallas_call(
        best_kernel,
        out_shape=jax.ShapeDtypeStruct((PLANES * COLUMNS, LANES), F32),
        in_specs=[VMEM],
        out_specs=VMEM,
        compiler_params=LIMIT,
        name="best",
    )(got.reshape(lines, LANES))
    owners = [
        [
            (spot % PLANES ^ PLANE_TURN) * COLUMNS + column_at(spot // PLANES)
            for spot in range(PLANES * COLUMNS)
        ]
    ]
    back = lax.all_to_all(
        best, ("z", "x", "core"), split_axis=0, concat_axis=0, tiled=True, axis_index_groups=owners
    )
    nearest = pl.pallas_call(
        finish_kernel,
        out_shape=jax.ShapeDtypeStruct((1, row_count), F32),
        in_specs=[VMEM, VMEM, VMEM],
        out_specs=VMEM,
        compiler_params=LIMIT,
        name="finish",
    )(back, target, live)
    return (prefix, nearest.reshape(row_count))


def solution(mesh):
    axes = ("z", "x", "core", "help")
    fine = Mesh(mesh.devices.reshape(PLANES, 4, 2, HELPERS), axes)
    return jax.shard_map(
        shards,
        mesh=fine,
        in_specs=(P(axes, None), P(), P(axes), P(), P(axes)),
        out_specs=(P(axes, None), P(axes)),
        check_vma=False,
    )
```

```python
import jax
import jax.numpy as jnp
from jax import lax
from jax.experimental import pallas as pl
from jax.experimental.pallas import tpu as pltpu
from jax.sharding import Mesh, PartitionSpec as P

NORM_EPS = 1e-06
LANES = 128
PLANES = 16
COLUMNS = 8
HELPERS = 4
SLOTS = 2
PLANE_SLOTS = COLUMNS * SLOTS
SLAB = PLANES * PLANE_SLOTS
OWNER_SLOTS = PLANES * SLOTS
CHUNK = 2 * OWNER_SLOTS + 2
PLANE_CHUNK = 2 * PLANE_SLOTS + 2
PLANE_TURN = 8
COLUMN_TURN = 5
HELPER_TURN = 2

F32 = jnp.float32
BF16 = jnp.bfloat16


def iota(shape, dim):
    return lax.broadcasted_iota(jnp.int32, shape, dim)


def column_at(place):
    return ((place & 3) * 2 + (place >> 2)) ^ COLUMN_TURN


def place_of(column):
    turned = column ^ COLUMN_TURN
    return (turned & 1) * 4 + (turned >> 1)


def hot(condition):
    return jnp.where(condition, 1.0, 0.0).astype(BF16)


def dot_nt(left, right):
    return lax.dot_general(left, right, (((1,), (1,)), ((), ())), preferred_element_type=F32)


def dot(left, right):
    return jnp.dot(left, right, preferred_element_type=F32)


def index_kernel(packed_ref, target_ref, hit_ref, label_ref):
    square = (LANES, LANES)
    cluster = packed_ref[16:17]
    high, low = cluster >> 7, cluster & 127
    by_low = dot(packed_ref[:16].astype(F32).astype(BF16), hot(iota(square, 0) == low))
    owner = jnp.sum(jnp.where(iota(by_low.shape, 0) == high, by_low, 0.0), axis=0, keepdims=True)
    owner = owner.astype(jnp.int32)
    owner_hot = hot(iota(square, 0) == owner)
    same = lax.dot_general(
        owner_hot, owner_hot, (((0,), (0,)), ((), ())), preferred_element_type=F32
    )
    slot = jnp.sum(jnp.where(iota(square, 0) < iota(square, 1), same, 0.0), axis=0, keepdims=True)
    target = owner * SLOTS + slot.astype(jnp.int32)
    target = target ^ (PLANE_TURN * PLANE_SLOTS)
    back = place_of((target >> 1) & 7) * OWNER_SLOTS + (target >> 4) * SLOTS + (target & 1)
    target_ref[...] = jnp.broadcast_to(back, target_ref.shape)

    live = packed_ref[17:18] == 1
    high_label = jnp.where(live, high + 1, 0)
    low_label = jnp.where(live, low, 0)
    line = iota(square, 0)
    part = jnp.where((line & 7) == 0, high_label, jnp.where((line & 7) == 1, low_label, 0))
    part = jnp.where((line >> 3) == (target >> 4), part, 0).astype(F32).astype(BF16)
    label_ref[...] = dot_nt(part, hot(line == (target & 15)))
    hit_ref[...] = hot(iota((SLAB, LANES), 0) == target)


def scatter_kernel(prefix_ref, hit_ref, label_ref, send_ref):
    rows = dot(hit_ref[...], prefix_ref[...]).astype(BF16)
    labels = label_ref[...].astype(BF16)
    parts = []
    for plane in range(PLANES):
        part = rows[plane * PLANE_SLOTS : (plane + 1) * PLANE_SLOTS]
        parts += [part[:, :LANES], part[:, LANES:], labels[plane * 8 : plane * 8 + 2]]
    send_ref[...] = jnp.concatenate(parts, axis=0)


def sort_kernel(got_ref, send_ref):
    helper = lax.axis_index("help") ^ HELPER_TURN
    got = got_ref[...]
    chunks = [got[plane * PLANE_CHUNK : (plane + 1) * PLANE_CHUNK] for plane in range(PLANES)]
    low = jnp.concatenate([chunk[:PLANE_SLOTS] for chunk in chunks], axis=0)
    high = jnp.concatenate([chunk[PLANE_SLOTS : 2 * PLANE_SLOTS] for chunk in chunks], axis=0)
    dest = iota((SLAB, SLAB), 0)
    source = (dest & 15) * PLANE_SLOTS + column_at(dest >> 5) * SLOTS + ((dest >> 4) & 1)
    order = hot(iota((SLAB, SLAB), 1) == source)
    rows = dot(order, jnp.concatenate([low, high], axis=1))
    rows = rows.reshape(COLUMNS, OWNER_SLOTS, 2 * LANES)

    tiles = jnp.concatenate([chunk[2 * PLANE_SLOTS :] for chunk in chunks], axis=0)
    line, lane = iota((2 * LANES, LANES), 0), iota((2 * LANES, LANES), 1)
    mine = ((line >> 5) & 3) == helper
    spread = dot(hot((lane == (line & 15) * 2 + (line >> 7)) & mine)[:, : 2 * PLANES], tiles)
    spread = jnp.where((lane & 1) == ((line >> 4) & 1), spread, 0.0).astype(BF16)
    group = (COLUMNS * 8, LANES)
    labels = dot_nt(hot((iota(group, 1) >> 1) == column_at(iota(group, 0) >> 3)), spread)
    labels = jnp.where((iota(group, 0) & 7) == 0, labels[:, :LANES], labels[:, LANES:])
    labels = labels.reshape(COLUMNS, 8, LANES)
    parts = []
    for column in range(COLUMNS):
        chunk = [rows[column, :, :LANES], rows[column, :, LANES:], labels[column, :2]]
        parts += [part.astype(BF16) for part in chunk] * HELPERS
    send_ref[...] = jnp.concatenate(parts, axis=0)


def best_kernel(got_ref, out_ref):
    helper = lax.axis_index("help") ^ HELPER_TURN
    got = got_ref[...]
    lows, highs, owns, labels = [], [], [], []
    for column in range(COLUMNS):
        own = label = None
        for place in range(HELPERS):
            start = (column * HELPERS + place) * CHUNK
            chunk = got[start : start + 2 * OWNER_SLOTS]
            lows.append(chunk[:OWNER_SLOTS])
            highs.append(chunk[OWNER_SLOTS:])
            own = chunk if own is None else jnp.where(helper == place, chunk, own)
            part = got[start + 2 * OWNER_SLOTS : start + CHUNK].astype(F32)
            label = part if label is None else label + part
        owns.append(own)
        labels.append(label[0:1] * 128.0 + label[1:2])
    columns = jnp.concatenate(
        [jnp.concatenate(lows, axis=0), jnp.concatenate(highs, axis=0)], axis=1
    )

    parts = [
        jnp.concatenate([own[part * PLANES : (part + 1) * PLANES] for own in owns], axis=0)
        for part in range(2 * SLOTS)
    ]
    own = jnp.concatenate(
        [jnp.concatenate(parts[:SLOTS], axis=0), jnp.concatenate(parts[SLOTS:], axis=0)], axis=1
    )
    scores = dot_nt(own, columns)

    label = jnp.concatenate(labels, axis=0).reshape(COLUMNS, 1, LANES)
    shape = (SLOTS, COLUMNS, PLANES, LANES)
    small = (SLOTS, 1, PLANES, LANES)
    self_lane = iota(small, 3) == helper * OWNER_SLOTS + iota(small, 0) * PLANES + iota(small, 2)
    spread = jnp.where(self_lane, label[None], 0.0)
    own_label = jnp.sum(spread, axis=3, keepdims=True)
    own_label = jnp.where(own_label > 0.5, own_label, -1.0)
    best = jnp.full(shape, -1.0, F32)
    for column in range(COLUMNS):
        block = scores[:, column * LANES : (column + 1) * LANES].reshape(shape)
        block = jnp.where(own_label == label[column][None, None], block, -1.0)
        no_self = jnp.where(self_lane, -1.0, block[:, column : column + 1])
        parts = [block[:, :column], no_self, block[:, column + 1 :]]
        best = jnp.maximum(best, jnp.concatenate([p for p in parts if p.shape[1]], axis=1))
    best = jnp.max(best, axis=3, keepdims=True).reshape(SLOTS, COLUMNS * PLANES, 1)
    lane = iota(out_ref.shape, 1)
    out_ref[...] = jnp.where(lane == 0, best[0], jnp.where(lane == 1, best[1], 0.0))


def finish_kernel(got_ref, target_ref, live_ref, out_ref):
    got = got_ref[...]
    target = target_ref[:1]
    value = jnp.where((target & 1) == 0, got[:, 0:1], got[:, 1:2])
    value = jnp.where(iota(got.shape, 0) == (target >> 1), value, 0.0)
    value = jnp.sum(value, axis=0, keepdims=True)
    out_ref[...] = jnp.where(live_ref[...] == 1, value, -1.0)


VMEM = pl.BlockSpec(memory_space=pltpu.VMEM)
LIMIT = pltpu.CompilerParams(vmem_limit_bytes=32 * 1024 * 1024)


def shards(embeds, head_rows, cluster_of, owner_of, live_mask):
    row_count = embeds.shape[0]
    live = live_mask.reshape(1, row_count)
    packed = jnp.concatenate([owner_of, cluster_of, live_mask]).reshape(-1, LANES)
    target, hit, label = pl.pallas_call(
        index_kernel,
        out_shape=(
            jax.ShapeDtypeStruct((8, row_count), jnp.int32),
            jax.ShapeDtypeStruct((SLAB, row_count), BF16),
            jax.ShapeDtypeStruct((PLANES * 8, LANES), F32),
        ),
        in_specs=[VMEM],
        out_specs=(VMEM,) * 3,
        compiler_params=LIMIT,
        cost_estimate=pl.CostEstimate(flops=700_000_000, bytes_accessed=0, transcendentals=0),
        name="index",
    )(packed)
    embeds, hit = lax.optimization_barrier((embeds, hit))
    projected = jnp.dot(embeds, head_rows, preferred_element_type=F32)
    norm = lax.rsqrt(jnp.sum(projected * projected, axis=1, keepdims=True) + NORM_EPS)
    prefix = (projected * norm).astype(BF16)
    send = pl.pallas_call(
        scatter_kernel,
        out_shape=jax.ShapeDtypeStruct((PLANES * PLANE_CHUNK, LANES), BF16),
        in_specs=[VMEM] * 3,
        out_specs=VMEM,
        compiler_params=LIMIT,
        name="scatter",
    )(prefix, hit, label)
    planes = [[spot ^ PLANE_TURN for spot in range(PLANES)]]
    send = send.reshape(PLANES, PLANE_CHUNK // 2, 2, LANES)
    got = lax.all_to_all(
        send, "z", split_axis=0, concat_axis=0, tiled=True, axis_index_groups=planes
    )
    lines = COLUMNS * HELPERS * CHUNK
    send = pl.pallas_call(
        sort_kernel,
        out_shape=jax.ShapeDtypeStruct((lines, LANES), BF16),
        in_specs=[VMEM],
        out_specs=VMEM,
        compiler_params=LIMIT,
        name="sort",
    )(got.reshape(PLANES * PLANE_CHUNK, LANES))
    members = [
        [
            column_at(spot // HELPERS) * HELPERS + (spot % HELPERS ^ HELPER_TURN)
            for spot in range(COLUMNS * HELPERS)
        ]
    ]
    got = lax.all_to_all(
        send.reshape(COLUMNS * HELPERS, CHUNK // 2, 2, LANES),
        ("x", "core", "help"),
        split_axis=0,
        concat_axis=0,
        tiled=True,
        axis_index_groups=members,
    )
    best = pl.pallas_call(
        best_kernel,
        out_shape=jax.ShapeDtypeStruct((PLANES * COLUMNS, LANES), F32),
        in_specs=[VMEM],
        out_specs=VMEM,
        compiler_params=LIMIT,
        name="best",
    )(got.reshape(lines, LANES))
    owners = [
        [
            (spot % PLANES ^ PLANE_TURN) * COLUMNS + column_at(spot // PLANES)
            for spot in range(PLANES * COLUMNS)
        ]
    ]
    back = lax.all_to_all(
        best, ("z", "x", "core"), split_axis=0, concat_axis=0, tiled=True, axis_index_groups=owners
    )
    nearest = pl.pallas_call(
        finish_kernel,
        out_shape=jax.ShapeDtypeStruct((1, row_count), F32),
        in_specs=[VMEM, VMEM, VMEM],
        out_specs=VMEM,
        compiler_params=LIMIT,
        name="finish",
    )(back, target, live)
    return (prefix, nearest.reshape(row_count))


def solution(mesh):
    axes = ("z", "x", "core", "help")
    fine = Mesh(mesh.devices.reshape(PLANES, 4, 2, HELPERS), axes)
    return jax.shard_map(
        shards,
        mesh=fine,
        in_specs=(P(axes, None), P(), P(axes), P(), P(axes)),
        out_specs=(P(axes, None), P(axes)),
        check_vma=False,
    )
```

```python
import jax
import jax.numpy as jnp
from jax import lax
from jax.experimental import pallas as pl
from jax.experimental.pallas import tpu as pltpu
from jax.sharding import Mesh, PartitionSpec as P

NORM_EPS = 1e-06
LANES = 128
PLANES = 16
COLUMNS = 8
HELPERS = 4
SLOTS = 2
PLANE_SLOTS = COLUMNS * SLOTS
SLAB = PLANES * PLANE_SLOTS
OWNER_SLOTS = PLANES * SLOTS
CHUNK = 2 * OWNER_SLOTS + 2
PLANE_CHUNK = 2 * PLANE_SLOTS + 2
PLANE_TURN = 8
COLUMN_TURN = 5
HELPER_TURN = 2

F32 = jnp.float32
BF16 = jnp.bfloat16


def iota(shape, dim):
    return lax.broadcasted_iota(jnp.int32, shape, dim)


def column_at(place):
    return ((place & 3) * 2 + (place >> 2)) ^ COLUMN_TURN


def place_of(column):
    turned = column ^ COLUMN_TURN
    return (turned & 1) * 4 + (turned >> 1)


def hot(condition):
    return jnp.where(condition, 1.0, 0.0).astype(BF16)


def dot_nt(left, right):
    return lax.dot_general(left, right, (((1,), (1,)), ((), ())), preferred_element_type=F32)


def dot(left, right):
    return jnp.dot(left, right, preferred_element_type=F32)


def index_kernel(packed_ref, target_ref, hit_ref, label_ref):
    square = (LANES, LANES)
    cluster = packed_ref[16:17]
    high, low = cluster >> 7, cluster & 127
    by_low = dot(packed_ref[:16].astype(F32).astype(BF16), hot(iota(square, 0) == low))
    owner = jnp.sum(jnp.where(iota(by_low.shape, 0) == high, by_low, 0.0), axis=0, keepdims=True)
    owner = owner.astype(jnp.int32)
    owner_hot = hot(iota(square, 0) == owner)
    same = lax.dot_general(
        owner_hot, owner_hot, (((0,), (0,)), ((), ())), preferred_element_type=F32
    )
    slot = jnp.sum(jnp.where(iota(square, 0) < iota(square, 1), same, 0.0), axis=0, keepdims=True)
    target = owner * SLOTS + slot.astype(jnp.int32)
    target = ((PLANE_TURN - (target >> 4)) & (PLANES - 1)) * PLANE_SLOTS + (target & (PLANE_SLOTS - 1))
    back = place_of((target >> 1) & 7) * OWNER_SLOTS + (target >> 4) * SLOTS + (target & 1)
    target_ref[...] = jnp.broadcast_to(back, target_ref.shape)

    live = packed_ref[17:18] == 1
    high_label = jnp.where(live, high + 1, 0)
    low_label = jnp.where(live, low, 0)
    line = iota(square, 0)
    part = jnp.where((line & 7) == 0, high_label, jnp.where((line & 7) == 1, low_label, 0))
    part = jnp.where((line >> 3) == (target >> 4), part, 0).astype(F32).astype(BF16)
    label_ref[...] = dot_nt(part, hot(line == (target & 15)))
    hit_ref[...] = hot(iota((SLAB, LANES), 0) == target)


def scatter_kernel(prefix_ref, hit_ref, label_ref, send_ref):
    rows = dot(hit_ref[...], prefix_ref[...]).astype(BF16)
    labels = label_ref[...].astype(BF16)
    parts = []
    for plane in range(PLANES):
        part = rows[plane * PLANE_SLOTS : (plane + 1) * PLANE_SLOTS]
        parts += [part[:, :LANES], part[:, LANES:], labels[plane * 8 : plane * 8 + 2]]
    send_ref[...] = jnp.concatenate(parts, axis=0)


def sort_kernel(got_ref, send_ref):
    helper = lax.axis_index("help") ^ HELPER_TURN
    got = got_ref[...]
    chunks = [got[plane * PLANE_CHUNK : (plane + 1) * PLANE_CHUNK] for plane in range(PLANES)]
    low = jnp.concatenate([chunk[:PLANE_SLOTS] for chunk in chunks], axis=0)
    high = jnp.concatenate([chunk[PLANE_SLOTS : 2 * PLANE_SLOTS] for chunk in chunks], axis=0)
    dest = iota((SLAB, SLAB), 0)
    source = (dest & 15) * PLANE_SLOTS + column_at(dest >> 5) * SLOTS + ((dest >> 4) & 1)
    order = hot(iota((SLAB, SLAB), 1) == source)
    rows = dot(order, jnp.concatenate([low, high], axis=1))
    rows = rows.reshape(COLUMNS, OWNER_SLOTS, 2 * LANES)

    tiles = jnp.concatenate([chunk[2 * PLANE_SLOTS :] for chunk in chunks], axis=0)
    line, lane = iota((2 * LANES, LANES), 0), iota((2 * LANES, LANES), 1)
    mine = ((line >> 5) & 3) == helper
    spread = dot(hot((lane == (line & 15) * 2 + (line >> 7)) & mine)[:, : 2 * PLANES], tiles)
    spread = jnp.where((lane & 1) == ((line >> 4) & 1), spread, 0.0).astype(BF16)
    group = (COLUMNS * 8, LANES)
    labels = dot_nt(hot((iota(group, 1) >> 1) == column_at(iota(group, 0) >> 3)), spread)
    labels = jnp.where((iota(group, 0) & 7) == 0, labels[:, :LANES], labels[:, LANES:])
    labels = labels.reshape(COLUMNS, 8, LANES)
    parts = []
    for column in range(COLUMNS):
        chunk = [rows[column, :, :LANES], rows[column, :, LANES:], labels[column, :2]]
        parts += [part.astype(BF16) for part in chunk] * HELPERS
    send_ref[...] = jnp.concatenate(parts, axis=0)


def best_kernel(got_ref, out_ref):
    helper = lax.axis_index("help") ^ HELPER_TURN
    got = got_ref[...]
    lows, highs, owns, labels = [], [], [], []
    for column in range(COLUMNS):
        own = label = None
        for place in range(HELPERS):
            start = (column * HELPERS + place) * CHUNK
            chunk = got[start : start + 2 * OWNER_SLOTS]
            lows.append(chunk[:OWNER_SLOTS])
            highs.append(chunk[OWNER_SLOTS:])
            own = chunk if own is None else jnp.where(helper == place, chunk, own)
            part = got[start + 2 * OWNER_SLOTS : start + CHUNK].astype(F32)
            label = part if label is None else label + part
        owns.append(own)
        labels.append(label[0:1] * 128.0 + label[1:2])
    columns = jnp.concatenate(
        [jnp.concatenate(lows, axis=0), jnp.concatenate(highs, axis=0)], axis=1
    )

    parts = [
        jnp.concatenate([own[part * PLANES : (part + 1) * PLANES] for own in owns], axis=0)
        for part in range(2 * SLOTS)
    ]
    own = jnp.concatenate(
        [jnp.concatenate(parts[:SLOTS], axis=0), jnp.concatenate(parts[SLOTS:], axis=0)], axis=1
    )
    scores = dot_nt(own, columns)

    label = jnp.concatenate(labels, axis=0).reshape(COLUMNS, 1, LANES)
    shape = (SLOTS, COLUMNS, PLANES, LANES)
    small = (SLOTS, 1, PLANES, LANES)
    self_lane = iota(small, 3) == helper * OWNER_SLOTS + iota(small, 0) * PLANES + iota(small, 2)
    spread = jnp.where(self_lane, label[None], 0.0)
    own_label = jnp.sum(spread, axis=3, keepdims=True)
    own_label = jnp.where(own_label > 0.5, own_label, -1.0)
    best = jnp.full(shape, -1.0, F32)
    for column in range(COLUMNS):
        block = scores[:, column * LANES : (column + 1) * LANES].reshape(shape)
        block = jnp.where(own_label == label[column][None, None], block, -1.0)
        no_self = jnp.where(self_lane, -1.0, block[:, column : column + 1])
        parts = [block[:, :column], no_self, block[:, column + 1 :]]
        best = jnp.maximum(best, jnp.concatenate([p for p in parts if p.shape[1]], axis=1))
    best = jnp.max(best, axis=3, keepdims=True).reshape(SLOTS, COLUMNS * PLANES, 1)
    lane = iota(out_ref.shape, 1)
    out_ref[...] = jnp.where(lane == 0, best[0], jnp.where(lane == 1, best[1], 0.0))


def finish_kernel(got_ref, target_ref, live_ref, out_ref):
    got = got_ref[...]
    target = target_ref[:1]
    value = jnp.where((target & 1) == 0, got[:, 0:1], got[:, 1:2])
    value = jnp.where(iota(got.shape, 0) == (target >> 1), value, 0.0)
    value = jnp.sum(value, axis=0, keepdims=True)
    out_ref[...] = jnp.where(live_ref[...] == 1, value, -1.0)


VMEM = pl.BlockSpec(memory_space=pltpu.VMEM)
LIMIT = pltpu.CompilerParams(vmem_limit_bytes=32 * 1024 * 1024)


def shards(embeds, head_rows, cluster_of, owner_of, live_mask):
    row_count = embeds.shape[0]
    live = live_mask.reshape(1, row_count)
    packed = jnp.concatenate([owner_of, cluster_of, live_mask]).reshape(-1, LANES)
    target, hit, label = pl.pallas_call(
        index_kernel,
        out_shape=(
            jax.ShapeDtypeStruct((8, row_count), jnp.int32),
            jax.ShapeDtypeStruct((SLAB, row_count), BF16),
            jax.ShapeDtypeStruct((PLANES * 8, LANES), F32),
        ),
        in_specs=[VMEM],
        out_specs=(VMEM,) * 3,
        compiler_params=LIMIT,
        cost_estimate=pl.CostEstimate(flops=700_000_000, bytes_accessed=0, transcendentals=0),
        name="index",
    )(packed)
    embeds, hit = lax.optimization_barrier((embeds, hit))
    projected = jnp.dot(embeds, head_rows, preferred_element_type=F32)
    norm = lax.rsqrt(jnp.sum(projected * projected, axis=1, keepdims=True) + NORM_EPS)
    prefix = (projected * norm).astype(BF16)
    send = pl.pallas_call(
        scatter_kernel,
        out_shape=jax.ShapeDtypeStruct((PLANES * PLANE_CHUNK, LANES), BF16),
        in_specs=[VMEM] * 3,
        out_specs=VMEM,
        compiler_params=LIMIT,
        name="scatter",
    )(prefix, hit, label)
    planes = [[(PLANE_TURN - spot) % PLANES for spot in range(PLANES)]]
    send = send.reshape(PLANES, PLANE_CHUNK // 2, 2, LANES)
    got = lax.all_to_all(
        send, "z", split_axis=0, concat_axis=0, tiled=True, axis_index_groups=planes
    )
    lines = COLUMNS * HELPERS * CHUNK
    send = pl.pallas_call(
        sort_kernel,
        out_shape=jax.ShapeDtypeStruct((lines, LANES), BF16),
        in_specs=[VMEM],
        out_specs=VMEM,
        compiler_params=LIMIT,
        name="sort",
    )(got.reshape(PLANES * PLANE_CHUNK, LANES))
    members = [
        [
            column_at(spot // HELPERS) * HELPERS + (spot % HELPERS ^ HELPER_TURN)
            for spot in range(COLUMNS * HELPERS)
        ]
    ]
    got = lax.all_to_all(
        send.reshape(COLUMNS * HELPERS, CHUNK // 2, 2, LANES),
        ("x", "core", "help"),
        split_axis=0,
        concat_axis=0,
        tiled=True,
        axis_index_groups=members,
    )
    best = pl.pallas_call(
        best_kernel,
        out_shape=jax.ShapeDtypeStruct((PLANES * COLUMNS, LANES), F32),
        in_specs=[VMEM],
        out_specs=VMEM,
        compiler_params=LIMIT,
        name="best",
    )(got.reshape(lines, LANES))
    owners = [
        [
            ((PLANE_TURN - spot) % PLANES) * COLUMNS + column_at(spot // PLANES)
            for spot in range(PLANES * COLUMNS)
        ]
    ]
    back = lax.all_to_all(
        best, ("z", "x", "core"), split_axis=0, concat_axis=0, tiled=True, axis_index_groups=owners
    )
    nearest = pl.pallas_call(
        finish_kernel,
        out_shape=jax.ShapeDtypeStruct((1, row_count), F32),
        in_specs=[VMEM, VMEM, VMEM],
        out_specs=VMEM,
        compiler_params=LIMIT,
        name="finish",
    )(back, target, live)
    return (prefix, nearest.reshape(row_count))


def solution(mesh):
    axes = ("z", "x", "core", "help")
    fine = Mesh(mesh.devices.reshape(PLANES, 4, 2, HELPERS), axes)
    return jax.shard_map(
        shards,
        mesh=fine,
        in_specs=(P(axes, None), P(), P(axes), P(), P(axes)),
        out_specs=(P(axes, None), P(axes)),
        check_vma=False,
    )
```
